512 devices in a mesh: tm: 8 (over x, y_hi), space: 64 (over z, y_lo, core).
Axes of the slice: x: 4, y: 4 (y_hi: 2, y_lo: 2; y = y_hi * 2 + y_lo), z: 16, core: 2. Of those that a mesh axis runs over, the one named last changes fastest.
Arguments:
- start_state: float32 [8, 2, 4096, 1024], P('tm', None, 'space'), may hold values from -6 to 6
- rigidity: float32 [4096, 1024], P('space'), may hold values from 0.5 to 2
- inv_mass: float32 [4096, 1024], P('space'), may hold values from 0.5 to 2
- gust_load: float32 [4096, 1024], P('space'), may hold values from -6 to 6
- kl_coeff: float32 [4, 4], replicated, may hold values from -3 to 3
- gust_history: float32 [32], P('tm'), may hold values from -4 to 4
Outputs:
- end_state: float32 [8, 2, 4096, 1024], P('tm', None, 'space')
The draws below stay inside these ranges and needn't reach their ends.
All inputs are finite; a program needn't handle non-finite values.
Results may differ from the reference program's by a relative error of at most 0.000082.
Values sent between devices are 32-bit elements; how exact they have to be, the bound alone decides.
A program may use at most 64 MiB of HBM per device.

```python
import math
import jax
import jax.numpy as jnp
from jax import lax

NY = 1024
FINE = 4
ITERS = 2
KL = 4
SLICES = 8
NX = 4096
STEPS = 32


def block_levels(own_key, shape, shards, low, top_value):
    def one(dim, shards_of):
        steps = jax.random.uniform(jax.random.fold_in(jax.random.fold_in(own_key, 6), dim), (shards_of,), jnp.float32, low / len(shards), top_value / len(shards))
        return jnp.repeat(jnp.exp(steps), shape[dim] // shards_of).reshape((-1,) + (1,) * (len(shape) - dim - 1))

    factor_of = one(*shards[0])
    for cut in shards[1:]:
        factor_of = factor_of * one(*cut)
    return factor_of


def scatter_about(own_key, dims, deviation, limit, shards=(), dtype=jnp.bfloat16):
    factor_of = block_levels(own_key, dims, shards, -0.22, 0.18) if shards else 1.0
    values = jax.random.normal(own_key, dims, jnp.float32) * deviation * factor_of
    return jnp.minimum(jnp.maximum(values, -limit), limit).astype(dtype)


def setup_inputs(seed: int = 0) -> dict:
    key_list = jax.random.split(jax.random.key(seed), 7)
    return {
        "start_state": scatter_about(key_list[0], (SLICES, 2, NX, NY), 1.0, 6.0, ((0, 8), (2, 64)), jnp.float32),
        "rigidity": jnp.clip(jnp.exp(math.log(2.0) - 1.3862944 * jax.random.uniform(key_list[1], (NX, NY), jnp.float32) ** block_levels(key_list[1], (NX, NY), ((0, 64),), -0.2, 0.2)), 0.5, 2.0),
        "inv_mass": jnp.clip(jnp.exp(math.log(2.0) - 1.3862944 * jax.random.uniform(key_list[2], (NX, NY), jnp.float32) ** block_levels(key_list[2], (NX, NY), ((0, 64),), -0.2, 0.2)), 0.5, 2.0),
        "gust_load": scatter_about(key_list[3], (NX, NY), 1.0, 6.0, ((0, 64),), jnp.float32),
        "kl_coeff": scatter_about(key_list[4], (KL, KL), 1.0, 3.0, (), jnp.float32),
        "gust_history": scatter_about(key_list[5], (STEPS,), 1.0, 4.0, ((0, 8),), jnp.float32),
    }


STIFF_SCALE = 1.0 / 64.0
TIME_STEP = 0.18
HALF_STEP = 0.09
DAMPING = 0.05


def laplace(padded):
    return padded[2:, 1:-1] + padded[:-2, 1:-1] + padded[1:-1, 2:] + padded[1:-1, :-2] - 4.0 * padded[1:-1, 1:-1]


def mode_table(positions, extent):
    orders = (jnp.arange(KL) + 1).astype(jnp.float32)
    coords = (positions.astype(jnp.float32) + 0.5) / extent
    return jnp.cos(jnp.pi * orders[:, None] * coords[None, :])


def build_rigidity(rigidity, kl_coeff, first_row, extent_rows, extent_cols):
    row_count = rigidity.shape[0]
    col_count = rigidity.shape[1]
    across = mode_table(first_row + jnp.arange(row_count).astype(jnp.int32), extent_rows)
    along_chord = mode_table(jnp.arange(col_count).astype(jnp.int32), extent_cols)
    mixed = jnp.dot(kl_coeff, along_chord, precision=lax.Precision.HIGHEST)
    kl_field = jnp.dot(across.T, mixed, precision=lax.Precision.HIGHEST)
    return rigidity * jnp.exp(0.5 * jnp.tanh(kl_field))


def stiffness(position, stiff_field):
    weighted = stiff_field * laplace(jnp.pad(position, 1))
    return STIFF_SCALE * laplace(jnp.pad(weighted, 1))


def accelerate(position, velocity, stiff_now, inv_mass, gust_load, gust_value):
    return inv_mass * (gust_load * gust_value - stiff_now) - DAMPING * velocity


def coarse_step(position, velocity, stiff_now, inv_mass, gust_load, gust_value):
    coarse_span = FINE * TIME_STEP
    new_vel = velocity + coarse_span * accelerate(position, velocity, stiff_now, inv_mass, gust_load, gust_value)
    return position + coarse_span * new_vel, new_vel


def fine_run(position, velocity, stiff_field, inv_mass, gust_load, gust_values):
    stiff_now = stiffness(position, stiff_field)
    first_stiff = stiff_now
    for step_index in range(FINE):
        gust_value = gust_values[step_index]
        half_vel = velocity + HALF_STEP * accelerate(position, velocity, stiff_now, inv_mass, gust_load, gust_value)
        position = position + TIME_STEP * half_vel
        stiff_now = stiffness(position, stiff_field)
        velocity = half_vel + HALF_STEP * accelerate(position, half_vel, stiff_now, inv_mass, gust_load, gust_value)
    return position, velocity, first_stiff


def reference(start_state, rigidity, inv_mass, gust_load, kl_coeff, gust_history):
    stiff_field = build_rigidity(rigidity, kl_coeff, 0, NX, NY)
    starts = [(start_state[slice_index, 0], start_state[slice_index, 1]) for slice_index in range(SLICES)]
    end_states = []
    for sweep_index in range(ITERS):
        deltas = []
        for slice_index in range(SLICES):
            values = gust_history[slice_index * FINE:(slice_index + 1) * FINE]
            base_pos, base_vel = starts[slice_index]
            fine_pos, fine_vel, first_stiff = fine_run(base_pos, base_vel, stiff_field, inv_mass, gust_load, values)
            coarse_pos, coarse_vel = coarse_step(base_pos, base_vel, first_stiff, inv_mass, gust_load, values[0])
            deltas.append((fine_pos - coarse_pos, fine_vel - coarse_vel))
        chain_pos, chain_vel = starts[0]
        end_states = []
        for slice_index in range(SLICES):
            stiff_now = stiffness(chain_pos, stiff_field)
            moved_pos, moved_vel = coarse_step(chain_pos, chain_vel, stiff_now, inv_mass, gust_load, gust_history[slice_index * FINE])
            chain_pos = moved_pos + deltas[slice_index][0]
            chain_vel = moved_vel + deltas[slice_index][1]
            end_states.append(jnp.stack([chain_pos, chain_vel]))
        starts = [starts[0]] + [(end_states[slice_index][0], end_states[slice_index][1]) for slice_index in range(SLICES - 1)]
    return jnp.stack(end_states)
```

```python
import functools

import jax
import jax.numpy as jnp
import numpy as np
from jax import lax
from jax.experimental import pallas as pl
from jax.experimental.pallas import tpu as pltpu
from jax.sharding import PartitionSpec as P

FINE = 4
KL = 4
STIFF_SCALE = 1.0 / 64.0
TIME_STEP = 0.18
HALF_STEP = 0.09
DAMPING = 0.05
COARSE = FINE * TIME_STEP
KEEP = 1.0 - HALF_STEP * DAMPING
KEEP_COARSE = 1.0 - COARSE * DAMPING
RATIO = COARSE / HALF_STEP

HALO = 32
STRIP = 128
ROWS = 64
REGION = STRIP + 2 * HALO
PAD = 8
HALF = REGION // 2
MESH = pl.DeviceIdType.MESH


def kernel(
    tcount,
    scount,
    state,
    rigidity,
    inv_mass,
    gust_load,
    kl_coeff,
    gust,
    cos_x,
    cos_y,
    out,
    state_v,
    coef_v,
    cosx_v,
    cosy_v,
    turned,
    halo_up,
    halo_down,
    coef_t,
    got_core,
    got_up,
    got_down,
    got_gust,
    coef_up,
    coef_down,
    gust_row,
    stiff,
    kick,
    load,
    pos,
    vel,
    weighted,
    diff_p,
    diff_q,
    first_k,
    corr,
    outgoing,
    incoming,
    result,
    local_sem,
    send_sem,
    recv_sem,
    coef_send,
    coef_recv,
    back_send,
    back_recv,
):
    t = lax.axis_index("tm")
    s = lax.axis_index("space")
    has_low = s > 0
    has_high = s < scount - 1
    last = tcount - 1

    load_state = pltpu.make_async_copy(state, state_v, local_sem.at[0])
    load_state.start()
    loads = [
        pltpu.make_async_copy(src, dst, local_sem.at[1 + i])
        for i, (src, dst) in enumerate(
            [
                (rigidity, coef_v.at[0]),
                (inv_mass, coef_v.at[1]),
                (gust_load, coef_v.at[2]),
                (cos_x.at[s], cosx_v),
                (cos_y.at[t], cosy_v),
            ]
        )
    ]
    for copy in loads:
        copy.start()

    barrier = pltpu.get_barrier_semaphore()

    def greet(tt, ss):
        pl.semaphore_signal(barrier, inc=1, device_id=(tt, ss), device_id_type=MESH)

    for i in range(1, tcount):
        greet(lax.rem(t + i, tcount), s)

    @pl.when(has_low)
    def _():
        for i in range(tcount):
            greet(lax.rem(t + i, tcount), s - 1)

    @pl.when(has_high)
    def _():
        for i in range(tcount):
            greet(lax.rem(t + i, tcount), s + 1)

    lane = lax.broadcasted_iota(jnp.int32, (8, 128), 1)

    def lanes(rows):
        return lax.broadcasted_iota(jnp.int32, (rows, 128), 1)

    zero_halo = jnp.zeros((HALO, 128), jnp.float32)
    turned[0:HALO, :] = zero_halo
    turned[HALO + tcount * STRIP :, :] = zero_halo
    load_state.wait()
    for i in range(tcount):
        turned[HALO + i * STRIP : HALO + (i + 1) * STRIP, :] = state_v[
            :, i * STRIP : (i + 1) * STRIP
        ].T

    row8 = lax.broadcasted_iota(jnp.int32, (8, 128), 0)
    gust_block = jnp.zeros((8, 128), jnp.float32)
    for i in range(FINE):
        gust_block = jnp.where(row8 == i, gust[i], gust_block)
    gust_row[...] = gust_block

    packed = halo_up.shape[0]
    first_quarter = lax.rem(lanes(packed), 64) < 32
    near = turned[0:packed, :]
    far = turned[HALF : HALF + packed, :]
    halo_up[...] = jnp.where(first_quarter, near, pltpu.roll(far, 32, 1))
    halo_down[...] = jnp.where(first_quarter, pltpu.roll(far, 96, 1), near)

    pl.semaphore_wait(
        barrier,
        tcount - 1 + tcount * has_low.astype(jnp.int32) + tcount * has_high.astype(jnp.int32),
    )

    def remote(src, dst, send, recv, tt, ss):
        return pltpu.make_async_remote_copy(
            src_ref=src,
            dst_ref=dst,
            send_sem=send,
            recv_sem=recv,
            device_id=(tt, ss),
            device_id_type=MESH,
        )

    def strip_of(tt, rows):
        return pl.ds(pl.multiple_of(tt * STRIP, STRIP), rows)

    def core_copy(tt, slot):
        return remote(
            turned.at[strip_of(tt, REGION)], got_core.at[slot], send_sem.at[0, tt], recv_sem.at[0, slot], tt, s
        )

    def up_copy(tt, slot):
        return remote(
            halo_up.at[strip_of(tt, HALF)], got_up.at[slot], send_sem.at[1, tt], recv_sem.at[1, slot], tt, s - 1
        )

    def down_copy(tt, slot):
        return remote(
            halo_down.at[strip_of(tt, HALF)], got_down.at[slot], send_sem.at[2, tt], recv_sem.at[2, slot], tt, s + 1
        )

    def gust_copy(tt, slot):
        return remote(gust_row, got_gust.at[slot], send_sem.at[3, tt], recv_sem.at[3, slot], tt, s)

    @pl.when(t < last)
    def _():
        for i in range(1, tcount + 1):
            tt = lax.rem(t + i, tcount)
            if i < tcount:
                core_copy(tt, t).start()

            @pl.when(has_low)
            def _():
                up_copy(tt, t).start()

            @pl.when(has_high)
            def _():
                down_copy(tt, t).start()

    for i in range(1, tcount):
        gust_copy(lax.rem(t + i, tcount), t).start()

    for copy in loads:
        copy.wait()

    def turn_coef(tile, first, rows, target):
        cols = pl.ds(pl.multiple_of(tile * STRIP, STRIP), STRIP)
        pair = jnp.concatenate([coef_v[0, :, cols], coef_v[1, :, cols]], axis=0).T
        other = jnp.concatenate([coef_v[2, :, cols], coef_v[2, :, cols]], axis=0).T
        coef_t[0, target : target + rows, :] = pair[first : first + rows]
        coef_t[1, target : target + rows, :] = other[first : first + rows]

    turn_coef(t, 0, STRIP, HALO)

    @pl.when(t > 0)
    def _():
        turn_coef(t - 1, STRIP - HALO, HALO, 0)

    @pl.when(t == 0)
    def _():
        coef_t[0, 0:HALO, :] = zero_halo
        coef_t[1, 0:HALO, :] = zero_halo

    @pl.when(t < last)
    def _():
        turn_coef(t + 1, 0, HALO, HALO + STRIP)

    @pl.when(t == last)
    def _():
        coef_t[0, HALO + STRIP :, :] = zero_halo
        coef_t[1, HALO + STRIP :, :] = zero_halo

    coef_low = remote(coef_t, coef_up, coef_send.at[0], coef_recv.at[0], t, s - 1)
    coef_high = remote(coef_t, coef_down, coef_send.at[1], coef_recv.at[1], t, s + 1)

    @pl.when(has_low)
    def _():
        coef_low.start()

    @pl.when(has_high)
    def _():
        coef_high.start()

    @pl.when(jnp.logical_not(has_low))
    def _():
        coef_down[...] = jnp.zeros_like(coef_down)
        got_down[...] = jnp.zeros_like(got_down)

    @pl.when(jnp.logical_not(has_high))
    def _():
        coef_up[...] = jnp.zeros_like(coef_up)
        got_up[...] = jnp.zeros_like(got_up)

    mixed = []
    for b in range(KL):
        row = kl_coeff[0, b] * cosx_v[0:1, :]
        for a in range(1, KL):
            row = row + kl_coeff[a, b] * cosx_v[a : a + 1, :]
        mixed.append(row)
    mixed = jnp.concatenate(mixed + [jnp.zeros((128 - KL, 128), jnp.float32)], axis=0)
    field = jnp.dot(
        cosy_v[...], mixed, precision=lax.Precision.HIGHEST, preferred_element_type=jnp.float32
    )
    factor = STIFF_SCALE * jnp.exp(0.5 * jnp.tanh(field))

    zero_pad = jnp.zeros((PAD, 128), jnp.float32)
    for buf in (pos, weighted, corr):
        for i in range(buf.shape[0]):
            buf[i, 0:PAD, :] = zero_pad
            buf[i, PAD + REGION :, :] = zero_pad
    for i in range(diff_p.shape[0]):
        diff_p[i, 0:PAD, :] = zero_pad
        diff_p[i, PAD + REGION :, :] = zero_pad

    @pl.when(has_high)
    def _():
        remote(coef_t, coef_up, coef_send.at[0], coef_recv.at[0], t, s + 1).wait_recv()

    @pl.when(has_low)
    def _():
        remote(coef_t, coef_down, coef_send.at[1], coef_recv.at[1], t, s - 1).wait_recv()

    all_lanes = lanes(REGION)
    core_lanes = all_lanes < ROWS
    up_lanes = all_lanes < ROWS + HALO

    def assemble(core, up, down):
        return jnp.where(core_lanes, core, jnp.where(up_lanes, up, down))

    own_pair, own_load = coef_t[0], coef_t[1]
    up_pair, up_load = coef_up[0], coef_up[1]
    down_pair, down_load = coef_down[0], coef_down[1]
    rig = assemble(own_pair, pltpu.roll(up_pair, 64, 1), pltpu.roll(down_pair, 64, 1))
    mass = assemble(pltpu.roll(own_pair, 64, 1), up_pair, down_pair)
    gload = assemble(own_load, up_load, down_load)
    stiff[...] = rig * factor
    kick[...] = HALF_STEP * mass
    load[...] = (HALF_STEP * mass) * gload

    def laplace(ref, slot, lo, hi):
        centre = ref[slot, PAD + lo : PAD + hi, :]
        rows = ref[slot, PAD + lo - 1 : PAD + hi - 1, :] + ref[slot, PAD + lo + 1 : PAD + hi + 1, :]
        sides = pltpu.roll(centre, 1, 1) + pltpu.roll(centre, 127, 1)
        return (rows + sides) - 4.0 * centre

    def stiffness(ref, slot, scratch, lo, hi):
        wlo, whi = max(lo - 8, 0), min(hi + 8, REGION)
        weighted[scratch, PAD + wlo : PAD + whi, :] = stiff[wlo:whi, :] * laplace(ref, slot, wlo, whi)
        return laplace(weighted, scratch, lo, hi)

    def fine(slot, scratch, spring, velocity, g, lows):
        lo = lows[0]
        hi = REGION - lo
        half = KEEP * velocity - kick[lo:hi, :] * spring + load[lo:hi, :] * g[0]
        pos[slot, PAD + lo : PAD + hi, :] += TIME_STEP * half
        vel[slot, lo:hi, :] = half
        for i in range(1, FINE):
            lo = lows[i]
            hi = REGION - lo
            spring = stiffness(pos, slot, scratch, lo, hi)
            half = (
                (KEEP * KEEP) * vel[slot, lo:hi, :]
                - (1.0 + KEEP) * (kick[lo:hi, :] * spring)
                + load[lo:hi, :] * (KEEP * g[i - 1] + g[i])
            )
            pos[slot, PAD + lo : PAD + hi, :] += TIME_STEP * half
            vel[slot, lo:hi, :] = half
        lo = lows[FINE]
        hi = REGION - lo
        spring = stiffness(pos, slot, scratch, lo, hi)
        return (
            pos[slot, PAD + lo : PAD + hi, :],
            KEEP * vel[slot, lo:hi, :] - kick[lo:hi, :] * spring + load[lo:hi, :] * g[FINE - 1],
        )

    def gusts(n):
        return [got_gust[n, i : i + 1, :] for i in range(FINE)]

    def own_copies():
        return (
            pltpu.make_async_copy(turned.at[strip_of(t, REGION)], got_core.at[t], local_sem.at[6]),
            pltpu.make_async_copy(gust_row, got_gust.at[t], local_sem.at[7]),
        )

    for copy in own_copies():
        copy.start()

    def first_sweep(i, carry):
        n = lax.rem(t - i + tcount, tcount)

        @pl.when(i > 0)
        def _():
            gust_copy(n, n).wait_recv()

        @pl.when(i == 0)
        def _():
            own_copies()[1].wait()
            own_copies()[0].wait()

        @pl.when(jnp.logical_and(i > 0, n < last))
        def _():
            core_copy(n, n).wait_recv()

        @pl.when(jnp.logical_and(has_high, n < last))
        def _():
            up_copy(n, n).wait_recv()

        @pl.when(jnp.logical_and(has_low, n < last))
        def _():
            down_copy(n, n).wait_recv()

        @pl.when(n < last)
        def _():
            sub = lanes(HALF)
            core_sub = sub < ROWS
            up_sub = sub < ROWS + HALO
            for part in range(2):
                first = part * HALF
                core = got_core[n, first : first + HALF, :]
                up = got_up[n]
                down = got_down[n]
                turn = [(64, 64, 0, 0), (32, 96, 96, 32)][part]
                p_up, p_down, q_up, q_down = [
                    v if k == 0 else pltpu.roll(v, k, 1)
                    for v, k in zip((up, down, up, down), turn)
                ]
                pos[0, PAD + first : PAD + first + HALF, :] = jnp.where(
                    core_sub, core, jnp.where(up_sub, p_up, p_down)
                )
                vel[0, first : first + HALF, :] = jnp.where(
                    core_sub, pltpu.roll(core, 64, 1), jnp.where(up_sub, q_up, q_down)
                )
            share = jnp.where(n > 0, 1.0, 0.0)
            spring = stiffness(pos, 0, 0, 0, REGION)
            coarse_q = KEEP_COARSE * vel[0] - RATIO * (kick[...] * spring)
            diff_q[n] = -share * coarse_q
            diff_p[n, PAD : PAD + REGION, :] = -share * (pos[0, PAD : PAD + REGION, :] + COARSE * coarse_q)
            new_p, new_q = fine(0, 0, spring, vel[0], gusts(n), (0, 0, 0, 8, 8))
            diff_p[n, PAD + 8 : PAD + REGION - 8, :] += new_p
            diff_q[n, 8 : REGION - 8, :] += new_q

        return carry

    lax.fori_loop(0, tcount, first_sweep, 0)

    def down8(value):
        return value // 8 * 8

    for n in range(1, tcount - 1):
        lo = down8(10 + 2 * n)
        hi = REGION - lo
        spring = stiffness(diff_p, n - 1, n % 2, lo, hi)
        first_k[n, lo:hi, :] = spring
        coarse_q = KEEP_COARSE * diff_q[n - 1, lo:hi, :] - RATIO * (kick[lo:hi, :] * spring)
        diff_q[n, lo:hi, :] += coarse_q
        diff_p[n, PAD + lo : PAD + hi, :] += diff_p[n - 1, PAD + lo : PAD + hi, :] + COARSE * coarse_q

    own = slice(HALO, HALO + STRIP)
    own_padded = slice(PAD + HALO, PAD + HALO + STRIP)
    own_lanes = lanes(STRIP) < ROWS

    def back_copy(n, slot):
        return remote(outgoing.at[n], incoming.at[slot], back_send.at[n], back_recv.at[slot], n, s)

    def send_back(n, p_own, q_own):
        outgoing[n] = jnp.where(own_lanes, p_own, pltpu.roll(q_own, 64, 1))

        @pl.when(t != n)
        def _():
            back_copy(n, t).start()

    send_back(0, diff_p[0, own_padded, :], diff_q[0, own, :])

    for n in range(1, tcount):
        slot = n % 2
        before = n - 1
        lows = [down8(10 + 2 * n + 2 * k) for k in range(FINE + 1)]
        lo = lows[0]
        hi = REGION - lo
        pos[slot, PAD + lo - 8 : PAD + hi + 8, :] = diff_p[before, PAD + lo - 8 : PAD + hi + 8, :]
        if n < tcount - 1:
            spring = first_k[n, lo:hi, :]
        else:
            spring = stiffness(pos, slot, slot, lo, hi)
        new_p, new_q = fine(slot, slot, spring, diff_q[before, lo:hi, :], gusts(n), lows)
        lo = lows[FINE]
        hi = REGION - lo
        if n > 1:
            spring = stiffness(corr, slot, 2, lo, hi)
            coarse_q = KEEP_COARSE * first_k[0, lo:hi, :] - RATIO * (kick[lo:hi, :] * spring)
            new_q = new_q + coarse_q
            new_p = new_p + (corr[slot, PAD + lo : PAD + hi, :] + COARSE * coarse_q)
        if n < tcount - 1:
            corr[1 - slot, PAD + lo : PAD + hi, :] = new_p - diff_p[n, PAD + lo : PAD + hi, :]
            first_k[0, lo:hi, :] = new_q - diff_q[n, lo:hi, :]
        off = HALO - lo
        send_back(n, new_p[off : off + STRIP], new_q[off : off + STRIP])

    def place(tt, block):
        cols = pl.ds(pl.multiple_of(tt * STRIP, STRIP), STRIP)
        result[:, cols] = block.T

    place(t, outgoing[t])
    for i in range(1, tcount):
        tt = lax.rem(t + i, tcount)
        back_copy(tt, tt).wait_recv()
        place(tt, incoming[tt])
    store = pltpu.make_async_copy(result, out, local_sem.at[0])
    store.start()

    for i in range(1, tcount):
        tt = lax.rem(t + i, tcount)
        back_copy(tt, t).wait_send()
        gust_copy(tt, t).wait_send()

    @pl.when(t < last)
    def _():
        for i in range(1, tcount + 1):
            tt = lax.rem(t + i, tcount)
            if i < tcount:
                core_copy(tt, t).wait_send()

            @pl.when(has_low)
            def _():
                up_copy(tt, t).wait_send()

            @pl.when(has_high)
            def _():
                down_copy(tt, t).wait_send()

    @pl.when(has_low)
    def _():
        coef_low.wait_send()

    @pl.when(has_high)
    def _():
        coef_high.wait_send()

    store.wait()


def tables(tcount, scount, rows, cols):
    orders = np.arange(1, KL + 1)
    lane = np.arange(128)
    along = np.where(lane < ROWS + HALO, lane, lane - 128)
    x = np.arange(scount)[:, None] * ROWS + along[None, :]
    y = np.arange(tcount)[:, None] * STRIP - HALO + np.arange(REGION)[None, :]
    cos_x = np.zeros((scount, 8, 128), np.float32)
    cos_x[:, :KL] = np.cos(np.pi * orders[None, :, None] * ((x[:, None, :] + 0.5) / rows))
    cos_y = np.zeros((tcount, REGION, 128), np.float32)
    cos_y[:, :, :KL] = np.cos(np.pi * orders[None, None, :] * ((y[:, :, None] + 0.5) / cols))
    return cos_x, cos_y


def per_device(tcount, scount, start_state, rigidity, inv_mass, gust_load, kl_coeff, gust_history):
    rows, cols = rigidity.shape
    cos_x, cos_y = tables(tcount, scount, rows * scount, cols)
    f32 = jnp.float32
    padded = PAD + REGION + PAD
    packed = (tcount - 1) * STRIP + HALF
    vmem = pltpu.VMEM
    dma = pltpu.SemaphoreType.DMA
    anywhere = pl.BlockSpec(memory_space=pl.ANY)
    scalars = pl.BlockSpec(memory_space=pltpu.SMEM)
    result = pl.pallas_call(
        functools.partial(kernel, tcount, scount),
        out_shape=jax.ShapeDtypeStruct((2 * rows, cols), f32),
        in_specs=[anywhere] * 4 + [scalars] * 2 + [anywhere] * 2,
        out_specs=anywhere,
        scratch_shapes=[
            vmem((2 * rows, cols), f32),
            vmem((3, rows, cols), f32),
            vmem((8, 128), f32),
            vmem((REGION, 128), f32),
            vmem((2 * HALO + tcount * STRIP, 128), f32),
            vmem((packed, 128), f32),
            vmem((packed, 128), f32),
            vmem((2, REGION, 128), f32),
            vmem((tcount, REGION, 128), f32),
            vmem((tcount, HALF, 128), f32),
            vmem((tcount, HALF, 128), f32),
            vmem((tcount, 8, 128), f32),
            vmem((2, REGION, 128), f32),
            vmem((2, REGION, 128), f32),
            vmem((8, 128), f32),
            vmem((REGION, 128), f32),
            vmem((REGION, 128), f32),
            vmem((REGION, 128), f32),
            vmem((2, padded, 128), f32),
            vmem((2, REGION, 128), f32),
            vmem((3, padded, 128), f32),
            vmem((tcount - 1, padded, 128), f32),
            vmem((tcount - 1, REGION, 128), f32),
            vmem((tcount - 1, REGION, 128), f32),
            vmem((2, padded, 128), f32),
            vmem((tcount, STRIP, 128), f32),
            vmem((tcount, STRIP, 128), f32),
            vmem((2 * rows, cols), f32),
            dma((8,)),
            dma((4, tcount)),
            dma((4, tcount)),
            dma((2,)),
            dma((2,)),
            dma((tcount,)),
            dma((tcount,)),
        ],
        compiler_params=pltpu.CompilerParams(
            collective_id=0, has_side_effects=True, vmem_limit_bytes=32 * 1024 * 1024
        ),
    )(
        start_state.reshape(2 * rows, cols),
        rigidity,
        inv_mass,
        gust_load,
        kl_coeff,
        gust_history,
        jnp.asarray(cos_x),
        jnp.asarray(cos_y),
    )
    return result.reshape(1, 2, rows, cols)


def solution(mesh):
    in_specs = (
        P("tm", None, "space", None),
        P("space", None),
        P("space", None),
        P("space", None),
        P(),
        P("tm"),
    )
    return jax.shard_map(
        functools.partial(per_device, mesh.shape["tm"], mesh.shape["space"]),
        mesh=mesh,
        in_specs=in_specs,
        out_specs=P("tm", None, "space", None),
        check_vma=False,
    )
```

```python
import functools

import jax
import jax.numpy as jnp
import numpy as np
from jax import lax
from jax.experimental import pallas as pl
from jax.experimental.pallas import tpu as pltpu
from jax.sharding import PartitionSpec as P

FINE = 4
KL = 4
STIFF_SCALE = 1.0 / 64.0
TIME_STEP = 0.18
HALF_STEP = 0.09
DAMPING = 0.05
COARSE = FINE * TIME_STEP
KEEP = 1.0 - HALF_STEP * DAMPING
KEEP_COARSE = 1.0 - COARSE * DAMPING
RATIO = COARSE / HALF_STEP

HALO = 32
STRIP = 128
ROWS = 64
REGION = STRIP + 2 * HALO
PAD = 8
HALF = REGION // 2
CHUNK = 32
MESH = pl.DeviceIdType.MESH


def chunks(lo, hi):
    return [(a, min(a + CHUNK, hi)) for a in range(lo, hi, CHUNK)]


def kernel(
    tcount,
    scount,
    state,
    rigidity,
    inv_mass,
    gust_load,
    kl_coeff,
    gust,
    cos_x,
    cos_y,
    out,
    state_v,
    coef_v,
    cosx_v,
    cosy_v,
    turned,
    halo,
    coef_t,
    coef_h,
    got_core,
    got_mate,
    got_far,
    got_gust,
    coef_mate,
    coef_far,
    gust_row,
    stiff,
    kick,
    load,
    pos,
    vel,
    weighted,
    diff_p,
    diff_q,
    corr_p,
    corr_q,
    outgoing,
    incoming,
    result,
    local_sem,
    send_sem,
    recv_sem,
    coef_send,
    coef_recv,
    back_send,
    back_recv,
):
    t = lax.axis_index("tm")
    s = lax.axis_index("space")
    last = tcount - 1
    core = lax.rem(s, 2)
    mate = s + 1 - 2 * core
    far = s - 1 + 2 * core
    has_far = jnp.logical_and(far >= 0, far < scount)

    load_state = pltpu.make_async_copy(state, state_v, local_sem.at[0])
    load_state.start()
    loads = [
        pltpu.make_async_copy(src, dst, local_sem.at[1 + i])
        for i, (src, dst) in enumerate(
            [
                (rigidity, coef_v.at[0]),
                (inv_mass, coef_v.at[1]),
                (gust_load, coef_v.at[2]),
                (cos_x.at[s], cosx_v),
                (cos_y.at[t], cosy_v),
            ]
        )
    ]
    for copy in loads:
        copy.start()

    barrier = pltpu.get_barrier_semaphore()

    def greet(tt, ss):
        pl.semaphore_signal(barrier, inc=1, device_id=(tt, ss), device_id_type=MESH)

    for i in range(1, tcount):
        greet(lax.rem(t + i, tcount), s)
    greet(t, mate)

    @pl.when(has_far)
    def _():
        for i in range(tcount):
            greet(lax.rem(t + i, tcount), far)

    def lanes(rows):
        return lax.broadcasted_iota(jnp.int32, (rows, 128), 1)

    def remote(src, dst, send, recv, tt, ss):
        return pltpu.make_async_remote_copy(
            src_ref=src,
            dst_ref=dst,
            send_sem=send,
            recv_sem=recv,
            device_id=(tt, ss),
            device_id_type=MESH,
        )

    def strip_of(tt, rows):
        return pl.ds(pl.multiple_of(tt * STRIP, STRIP), rows)

    def core_copy(tt, slot):
        return remote(
            turned.at[strip_of(tt, REGION)], got_core.at[slot], send_sem.at[0, tt], recv_sem.at[0, slot], tt, s
        )

    def far_copy(tt, slot):
        return remote(
            halo.at[strip_of(tt, HALF)], got_far.at[slot], send_sem.at[1, tt], recv_sem.at[1, slot], tt, far
        )

    def mate_copy(slot):
        return remote(
            got_core.at[slot], got_mate.at[slot], send_sem.at[2, slot], recv_sem.at[2, slot], t, mate
        )

    def gust_copy(tt, slot):
        return remote(gust_row, got_gust.at[slot], send_sem.at[3, tt], recv_sem.at[3, slot], tt, s)

    coef_near = remote(coef_t, coef_mate, coef_send.at[0], coef_recv.at[0], t, mate)
    coef_away = remote(coef_h, coef_far, coef_send.at[1], coef_recv.at[1], t, far)
    own_copy = pltpu.make_async_copy(turned.at[strip_of(t, REGION)], got_core.at[t], local_sem.at[6])
    own_gust = pltpu.make_async_copy(gust_row, got_gust.at[t], local_sem.at[7])

    zero_halo = jnp.zeros((HALO, 128), jnp.float32)
    turned[0:HALO, :] = zero_halo
    turned[HALO + tcount * STRIP :, :] = zero_halo
    load_state.wait()
    for i in range(tcount):
        turned[HALO + i * STRIP : HALO + (i + 1) * STRIP, :] = state_v[
            :, i * STRIP : (i + 1) * STRIP
        ].T
    row8 = lax.broadcasted_iota(jnp.int32, (8, 128), 0)
    gust_block = jnp.zeros((8, 128), jnp.float32)
    for i in range(FINE):
        gust_block = jnp.where(row8 == i, gust[i], gust_block)
    gust_row[...] = gust_block

    def pack(near, further):
        upper = lax.rem(lanes(near.shape[0]), 64) >= 32
        return jnp.where(
            core == 0,
            jnp.where(upper, pltpu.roll(further, 32, 1), near),
            jnp.where(upper, near, pltpu.roll(further, 96, 1)),
        )

    for a, b in chunks(0, halo.shape[0]):
        halo[a:b, :] = pack(turned[a:b, :], turned[HALF + a : HALF + b, :])

    pl.semaphore_wait(barrier, tcount + tcount * has_far.astype(jnp.int32))

    def send_to(i):
        tt = lax.rem(t + i, tcount)
        if i < tcount:
            gust_copy(tt, t).start()

            @pl.when(t < last)
            def _():
                core_copy(tt, t).start()

        @pl.when(jnp.logical_and(t < last, has_far))
        def _():
            far_copy(tt, t).start()

    own_copy.start()
    own_gust.start()
    send_to(tcount)
    send_to(1)

    for copy in loads:
        copy.wait()

    def turn_coef(tile, first, rows, target):
        cols = pl.ds(pl.multiple_of(tile * STRIP, STRIP), STRIP)
        pair = jnp.concatenate([coef_v[0, :, cols], coef_v[1, :, cols]], axis=0).T
        other = jnp.concatenate([coef_v[2, :, cols], coef_v[2, :, cols]], axis=0).T
        coef_t[0, target : target + rows, :] = pair[first : first + rows]
        coef_t[1, target : target + rows, :] = other[first : first + rows]

    turn_coef(t, 0, STRIP, HALO)

    @pl.when(t > 0)
    def _():
        turn_coef(t - 1, STRIP - HALO, HALO, 0)

    @pl.when(t == 0)
    def _():
        coef_t[0, 0:HALO, :] = zero_halo
        coef_t[1, 0:HALO, :] = zero_halo

    @pl.when(t < last)
    def _():
        turn_coef(t + 1, 0, HALO, HALO + STRIP)

    @pl.when(t == last)
    def _():
        coef_t[0, HALO + STRIP :, :] = zero_halo
        coef_t[1, HALO + STRIP :, :] = zero_halo

    for k in range(2):
        coef_h[k] = pack(coef_t[k, 0:HALF, :], coef_t[k, HALF:, :])

    coef_near.start()

    @pl.when(has_far)
    def _():
        coef_away.start()

    for i in range(2, tcount):
        send_to(i)

    own_copy.wait()

    @pl.when(t < last)
    def _():
        mate_copy(t).start()

    @pl.when(jnp.logical_not(has_far))
    def _():
        coef_far[...] = jnp.zeros_like(coef_far)
        got_far[...] = jnp.zeros_like(got_far)

    mixed = []
    for b in range(KL):
        row = kl_coeff[0, b] * cosx_v[0:1, :]
        for a in range(1, KL):
            row = row + kl_coeff[a, b] * cosx_v[a : a + 1, :]
        mixed.append(row)
    mixed = jnp.concatenate(mixed + [jnp.zeros((128 - KL, 128), jnp.float32)], axis=0)
    field = jnp.dot(
        cosy_v[...], mixed, precision=lax.Precision.HIGHEST, preferred_element_type=jnp.float32
    )
    stiff[...] = STIFF_SCALE * jnp.exp(0.5 * jnp.tanh(field))

    zero_pad = jnp.zeros((PAD, 128), jnp.float32)
    for buf in (pos, weighted, corr_p, diff_p):
        for i in range(buf.shape[0]):
            buf[i, 0:PAD, :] = zero_pad
            buf[i, PAD + REGION :, :] = zero_pad

    def first_values(own, by_mate, by_far):
        lane = lanes(own.shape[0])
        from_mate = jnp.logical_and(lane >= 64 + 32 * core, lane < 96 + 32 * core)
        return jnp.where(lane < ROWS, own, jnp.where(from_mate, pltpu.roll(by_mate, 64, 1), by_far))

    def second_values(own, by_mate, by_far):
        lane = lanes(own.shape[0])
        from_mate = jnp.logical_and(lane >= 64 + 32 * core, lane < 96 + 32 * core)
        return jnp.where(lane < ROWS, pltpu.roll(own, 64, 1), jnp.where(from_mate, by_mate, by_far))

    def unpack(block, part):
        if part == 0:
            return pltpu.roll(block, 64, 1), block
        right, left = pltpu.roll(block, 32, 1), pltpu.roll(block, 96, 1)
        return jnp.where(core == 1, right, left), jnp.where(core == 1, left, right)

    coef_near.wait_recv()

    @pl.when(has_far)
    def _():
        coef_away.wait_recv()

    for part in range(2):
        for a, b in chunks(0, HALF):
            rows = slice(part * HALF + a, part * HALF + b)
            far_rig, far_mass = unpack(coef_far[0, a:b, :], part)
            far_load, _ = unpack(coef_far[1, a:b, :], part)
            rig = first_values(coef_t[0, rows, :], coef_mate[0, rows, :], far_rig)
            mass = HALF_STEP * second_values(coef_t[0, rows, :], coef_mate[0, rows, :], far_mass)
            stiff[rows, :] *= rig
            kick[0, rows, :] = mass
            kick[1, rows, :] = (1.0 + KEEP) * mass
            kick[2, rows, :] = RATIO * mass
            load[rows, :] = mass * first_values(coef_t[1, rows, :], coef_mate[1, rows, :], far_load)

    def laplace(ref, slot, a, b):
        centre = ref[slot, PAD + a : PAD + b, :]
        rows = ref[slot, PAD + a - 1 : PAD + b - 1, :] + ref[slot, PAD + a + 1 : PAD + b + 1, :]
        sides = pltpu.roll(centre, 1, 1) + pltpu.roll(centre, 127, 1)
        return (rows + sides) - 4.0 * centre

    def stencil(ref, slot, scratch, lo, finish):
        hi = REGION - lo
        ahead = chunks(max(lo - 8, 0), min(hi + 8, REGION))
        for a, b in chunks(lo, hi):
            while ahead and ahead[0][0] < b + 8:
                c, d = ahead.pop(0)
                weighted[scratch, PAD + c : PAD + d, :] = stiff[c:d, :] * laplace(ref, slot, c, d)
            finish(a, b, laplace(weighted, scratch, a, b))

    def fine_tail(slot, scratch, g, lows, finish):
        for i in range(1, FINE):
            push = KEEP * g[i - 1] + g[i]

            def move(a, b, spring, push=push):
                half = (
                    (KEEP * KEEP) * vel[slot, a:b, :] - kick[1, a:b, :] * spring + load[a:b, :] * push
                )
                pos[slot, PAD + a : PAD + b, :] += TIME_STEP * half
                vel[slot, a:b, :] = half

            stencil(pos, slot, scratch, lows[i], move)

        def close(a, b, spring):
            finish(
                a,
                b,
                pos[slot, PAD + a : PAD + b, :],
                KEEP * vel[slot, a:b, :] - kick[0, a:b, :] * spring + load[a:b, :] * g[FINE - 1],
            )

        stencil(pos, slot, scratch, lows[FINE], close)

    def gusts(n):
        return [got_gust[n, i : i + 1, :] for i in range(FINE)]

    def forward(i):
        n = lax.rem(t - i + tcount, tcount)

        @pl.when(n < last)
        def _():
            core_copy(n, n).wait_recv()
            mate_copy(n).start()

    forward(1)

    def first_sweep(i, carry):
        n = lax.rem(t - i + tcount, tcount)

        @pl.when(jnp.logical_and(i > 0, i < last))
        def _():
            forward(i + 1)

        @pl.when(i > 0)
        def _():
            gust_copy(n, n).wait_recv()

        @pl.when(i == 0)
        def _():
            own_gust.wait()

        @pl.when(jnp.logical_and(has_far, n < last))
        def _():
            far_copy(n, n).wait_recv()

        @pl.when(n < last)
        def _():
            mate_copy(n).wait_recv()
            for part in range(2):
                for a, b in chunks(0, HALF):
                    c, d = part * HALF + a, part * HALF + b
                    p_far, q_far = unpack(got_far[n, a:b, :], part)
                    own = got_core[n, c:d, :]
                    other = got_mate[n, c:d, :]
                    pos[0, PAD + c : PAD + d, :] = first_values(own, other, p_far)
                    vel[0, c:d, :] = second_values(own, other, q_far)
            share = jnp.where(n > 0, 1.0, 0.0)
            g = gusts(n)

            def begin(a, b, spring):
                p = pos[0, PAD + a : PAD + b, :]
                q = vel[0, a:b, :]
                coarse_q = KEEP_COARSE * q - kick[2, a:b, :] * spring
                diff_q[n, a:b, :] = -share * coarse_q
                diff_p[n, PAD + a : PAD + b, :] = -share * (p + COARSE * coarse_q)
                half = KEEP * q - kick[0, a:b, :] * spring + load[a:b, :] * g[0]
                pos[0, PAD + a : PAD + b, :] = p + TIME_STEP * half
                vel[0, a:b, :] = half

            def end(a, b, new_p, new_q):
                diff_p[n, PAD + a : PAD + b, :] += new_p
                diff_q[n, a:b, :] += new_q

            stencil(pos, 0, 0, 0, begin)
            fine_tail(0, 0, g, (0, 0, 0, 8, 8), end)

        return carry

    lax.fori_loop(0, tcount, first_sweep, 0)

    def back_copy(n, slot):
        return remote(outgoing.at[n], incoming.at[slot], back_send.at[n], back_recv.at[slot], n, s)

    def stage(n, a, b, p, q):
        first, end = max(a, HALO), min(b, HALO + STRIP)
        if first < end:
            outgoing[n, first - HALO : end - HALO, :] = jnp.where(
                lanes(end - first) < ROWS,
                p[first - a : end - a],
                pltpu.roll(q[first - a : end - a], 64, 1),
            )

    def send_back(n):
        @pl.when(t != n)
        def _():
            back_copy(n, t).start()

    for a, b in chunks(HALO, HALO + STRIP):
        stage(0, a, b, diff_p[0, PAD + a : PAD + b, :], diff_q[0, a:b, :])
    send_back(0)

    for n in range(1, tcount):
        slot = n % 2
        lows = [(10 + 2 * n + 2 * k) // 8 * 8 for k in range(FINE + 1)]
        g = gusts(n)

        def begin(a, b, spring, n=n, slot=slot, g=g):
            p = diff_p[n - 1, PAD + a : PAD + b, :]
            q = diff_q[n - 1, a:b, :]
            if n < last:
                coarse_q = KEEP_COARSE * q - kick[2, a:b, :] * spring
                diff_q[n, a:b, :] += coarse_q
                diff_p[n, PAD + a : PAD + b, :] += p + COARSE * coarse_q
            half = KEEP * q - kick[0, a:b, :] * spring + load[a:b, :] * g[0]
            pos[slot, PAD + a : PAD + b, :] = p + TIME_STEP * half
            vel[slot, a:b, :] = half

        stencil(diff_p, n - 1, 2 + slot, lows[0], begin)

        if n > 1:

            def correct(a, b, spring, slot=slot):
                coarse_q = KEEP_COARSE * corr_q[slot, a:b, :] - kick[2, a:b, :] * spring
                corr_q[slot, a:b, :] = coarse_q
                corr_p[slot, PAD + a : PAD + b, :] += COARSE * coarse_q

            stencil(corr_p, slot, 4, lows[FINE], correct)

        def end(a, b, new_p, new_q, n=n, slot=slot):
            if n > 1:
                new_p = new_p + corr_p[slot, PAD + a : PAD + b, :]
                new_q = new_q + corr_q[slot, a:b, :]
            if n < last:
                corr_p[1 - slot, PAD + a : PAD + b, :] = new_p - diff_p[n, PAD + a : PAD + b, :]
                corr_q[1 - slot, a:b, :] = new_q - diff_q[n, a:b, :]
            stage(n, a, b, new_p, new_q)

        fine_tail(slot, slot, g, lows, end)
        send_back(n)

    def place(tt, block):
        cols = pl.ds(pl.multiple_of(tt * STRIP, STRIP), STRIP)
        result[:, cols] = block.T

    place(t, outgoing[t])
    for i in range(1, tcount):
        tt = lax.rem(t + i, tcount)
        back_copy(tt, tt).wait_recv()
        place(tt, incoming[tt])
    store = pltpu.make_async_copy(result, out, local_sem.at[0])
    store.start()

    for i in range(1, tcount + 1):
        tt = lax.rem(t + i, tcount)
        if i < tcount:
            back_copy(tt, t).wait_send()
            gust_copy(tt, t).wait_send()

            @pl.when(t < last)
            def _():
                core_copy(tt, t).wait_send()

        @pl.when(tt < last)
        def _():
            mate_copy(tt).wait_send()

        @pl.when(jnp.logical_and(t < last, has_far))
        def _():
            far_copy(tt, t).wait_send()

    coef_near.wait_send()

    @pl.when(has_far)
    def _():
        coef_away.wait_send()

    store.wait()


def tables(tcount, scount, rows, cols):
    orders = np.arange(1, KL + 1)
    lane = np.arange(128)
    along = np.where(lane < ROWS + HALO, lane, lane - 128)
    x = np.arange(scount)[:, None] * ROWS + along[None, :]
    y = np.arange(tcount)[:, None] * STRIP - HALO + np.arange(REGION)[None, :]
    cos_x = np.zeros((scount, 8, 128), np.float32)
    cos_x[:, :KL] = np.cos(np.pi * orders[None, :, None] * ((x[:, None, :] + 0.5) / rows))
    cos_y = np.zeros((tcount, REGION, 128), np.float32)
    cos_y[:, :, :KL] = np.cos(np.pi * orders[None, None, :] * ((y[:, :, None] + 0.5) / cols))
    return cos_x, cos_y


def per_device(tcount, scount, start_state, rigidity, inv_mass, gust_load, kl_coeff, gust_history):
    rows, cols = rigidity.shape
    cos_x, cos_y = tables(tcount, scount, rows * scount, cols)
    f32 = jnp.float32
    padded = PAD + REGION + PAD
    packed = (tcount - 1) * STRIP + HALF
    vmem = pltpu.VMEM
    dma = pltpu.SemaphoreType.DMA
    hbm = pl.BlockSpec(memory_space=pltpu.HBM)
    scalars = pl.BlockSpec(memory_space=pltpu.SMEM)
    result = pl.pallas_call(
        functools.partial(kernel, tcount, scount),
        out_shape=jax.ShapeDtypeStruct((2 * rows, cols), f32),
        in_specs=[hbm] * 4 + [scalars] * 2 + [hbm] * 2,
        out_specs=hbm,
        scratch_shapes=[
            vmem((2 * rows, cols), f32),
            vmem((3, rows, cols), f32),
            vmem((8, 128), f32),
            vmem((REGION, 128), f32),
            vmem((2 * HALO + tcount * STRIP, 128), f32),
            vmem((packed, 128), f32),
            vmem((2, REGION, 128), f32),
            vmem((2, HALF, 128), f32),
            vmem((tcount, REGION, 128), f32),
            vmem((tcount, REGION, 128), f32),
            vmem((tcount, HALF, 128), f32),
            vmem((tcount, 8, 128), f32),
            vmem((2, REGION, 128), f32),
            vmem((2, HALF, 128), f32),
            vmem((8, 128), f32),
            vmem((REGION, 128), f32),
            vmem((3, REGION, 128), f32),
            vmem((REGION, 128), f32),
            vmem((2, padded, 128), f32),
            vmem((2, REGION, 128), f32),
            vmem((5, padded, 128), f32),
            vmem((tcount - 1, padded, 128), f32),
            vmem((tcount - 1, REGION, 128), f32),
            vmem((2, padded, 128), f32),
            vmem((2, REGION, 128), f32),
            vmem((tcount, STRIP, 128), f32),
            vmem((tcount, STRIP, 128), f32),
            vmem((2 * rows, cols), f32),
            dma((8,)),
            dma((4, tcount)),
            dma((4, tcount)),
            dma((2,)),
            dma((2,)),
            dma((tcount,)),
            dma((tcount,)),
        ],
        compiler_params=pltpu.CompilerParams(
            collective_id=0, has_side_effects=True, vmem_limit_bytes=60 * 1024 * 1024
        ),
    )(
        start_state.reshape(2 * rows, cols),
        rigidity,
        inv_mass,
        gust_load,
        kl_coeff,
        gust_history,
        jnp.asarray(cos_x),
        jnp.asarray(cos_y),
    )
    return result.reshape(1, 2, rows, cols)


def solution(mesh):
    in_specs = (
        P("tm", None, "space", None),
        P("space", None),
        P("space", None),
        P("space", None),
        P(),
        P("tm"),
    )
    return jax.shard_map(
        functools.partial(per_device, mesh.shape["tm"], mesh.shape["space"]),
        mesh=mesh,
        in_specs=in_specs,
        out_specs=P("tm", None, "space", None),
        check_vma=False,
    )
```

```python
import functools

import jax
import jax.numpy as jnp
import numpy as np
from jax import lax
from jax.experimental import pallas as pl
from jax.experimental.pallas import tpu as pltpu
from jax.sharding import PartitionSpec as P

FINE = 4
KL = 4
STIFF_SCALE = 1.0 / 64.0
TIME_STEP = 0.18
HALF_STEP = 0.09
DAMPING = 0.05
COARSE = FINE * TIME_STEP
KEEP = 1.0 - HALF_STEP * DAMPING
KEEP_COARSE = 1.0 - COARSE * DAMPING
RATIO = COARSE / HALF_STEP

HALO = 32
STRIP = 128
ROWS = 64
REGION = STRIP + 2 * HALO
PAD = 8
HALF = REGION // 2
CHUNK = 32
MESH = pl.DeviceIdType.MESH


def chunks(lo, hi):
    return [(a, min(a + CHUNK, hi)) for a in range(lo, hi, CHUNK)]


def kernel(
    tcount,
    scount,
    state,
    rigidity,
    inv_mass,
    gust_load,
    kl_coeff,
    gust,
    cos_x,
    cos_y,
    out,
    state_v,
    coef_v,
    kl_v,
    gust_v,
    cosx_v,
    cosy_v,
    turned,
    halo,
    coef_t,
    coef_h,
    got_core,
    got_mate,
    got_far,
    got_gust,
    coef_mate,
    coef_far,
    gust_row,
    stiff,
    kick,
    load,
    pos,
    vel,
    weighted,
    diff_p,
    diff_q,
    corr_p,
    corr_q,
    outgoing,
    incoming,
    local_sem,
    send_sem,
    recv_sem,
    coef_send,
    coef_recv,
    back_send,
    back_recv,
):
    t = lax.axis_index("tm")
    s = lax.axis_index("space")
    last = tcount - 1
    core = lax.rem(s, 2)
    mate = s + 1 - 2 * core
    far = s - 1 + 2 * core
    has_far = jnp.logical_and(far >= 0, far < scount)

    load_state = pltpu.make_async_copy(state, state_v, local_sem.at[0])
    load_state.start()
    load_gust = pltpu.make_async_copy(gust, gust_v, local_sem.at[9])
    load_gust.start()
    loads = [
        pltpu.make_async_copy(src, dst, local_sem.at[1 + i])
        for i, (src, dst) in enumerate(
            [
                (rigidity, coef_v.at[0]),
                (inv_mass, coef_v.at[1]),
                (gust_load, coef_v.at[2]),
                (cos_x.at[s], cosx_v),
                (cos_y.at[t], cosy_v),
                (kl_coeff, kl_v),
            ]
        )
    ]
    for copy in loads:
        copy.start()

    barrier = pltpu.get_barrier_semaphore()

    def greet(tt, ss):
        pl.semaphore_signal(barrier, inc=1, device_id=(tt, ss), device_id_type=MESH)

    for i in range(1, tcount):
        greet(lax.rem(t + i, tcount), s)
    greet(t, mate)

    @pl.when(has_far)
    def _():
        for i in range(tcount):
            greet(lax.rem(t + i, tcount), far)

    def lanes(rows):
        return lax.broadcasted_iota(jnp.int32, (rows, 128), 1)

    def remote(src, dst, send, recv, tt, ss):
        return pltpu.make_async_remote_copy(
            src_ref=src,
            dst_ref=dst,
            send_sem=send,
            recv_sem=recv,
            device_id=(tt, ss),
            device_id_type=MESH,
        )

    def strip_of(tt, rows):
        return pl.ds(pl.multiple_of(tt * STRIP, STRIP), rows)

    def core_copy(tt, slot):
        return remote(
            turned.at[strip_of(tt, REGION)], got_core.at[slot], send_sem.at[0, tt], recv_sem.at[0, slot], tt, s
        )

    def far_copy(tt, slot):
        return remote(
            halo.at[strip_of(tt, HALF)], got_far.at[slot], send_sem.at[1, tt], recv_sem.at[1, slot], tt, far
        )

    def mate_copy(slot):
        return remote(
            got_core.at[slot], got_mate.at[slot], send_sem.at[2, slot], recv_sem.at[2, slot], t, mate
        )

    def gust_copy(tt, slot):
        return remote(gust_row, got_gust.at[slot], send_sem.at[3, tt], recv_sem.at[3, slot], tt, s)

    coef_near = remote(coef_t, coef_mate, coef_send.at[0], coef_recv.at[0], t, mate)
    coef_away = remote(coef_h, coef_far, coef_send.at[1], coef_recv.at[1], t, far)
    own_copy = pltpu.make_async_copy(turned.at[strip_of(t, REGION)], got_core.at[t], local_sem.at[7])
    own_gust = pltpu.make_async_copy(gust_row, got_gust.at[t], local_sem.at[8])

    zero_halo = jnp.zeros((HALO, 128), jnp.float32)
    turned[0:HALO, :] = zero_halo
    turned[HALO + tcount * STRIP :, :] = zero_halo
    load_state.wait()
    load_gust.wait()
    for i in range(tcount):
        turned[HALO + i * STRIP : HALO + (i + 1) * STRIP, :] = state_v[
            :, i * STRIP : (i + 1) * STRIP
        ].T
    row8 = lax.broadcasted_iota(jnp.int32, (8, 128), 0)
    gust_block = jnp.zeros((8, 128), jnp.float32)
    for i in range(FINE):
        gust_block = jnp.where(row8 == i, gust_v[0:1, i : i + 1], gust_block)
    gust_row[...] = gust_block

    def pack(near, further):
        upper = lax.rem(lanes(near.shape[0]), 64) >= 32
        return jnp.where(
            core == 0,
            jnp.where(upper, pltpu.roll(further, 32, 1), near),
            jnp.where(upper, near, pltpu.roll(further, 96, 1)),
        )

    for a, b in chunks(0, halo.shape[0]):
        halo[a:b, :] = pack(turned[a:b, :], turned[HALF + a : HALF + b, :])

    pl.semaphore_wait(barrier, tcount + tcount * has_far.astype(jnp.int32))

    def send_to(i):
        tt = lax.rem(t + i, tcount)
        if i < tcount:
            gust_copy(tt, t).start()

            @pl.when(t < last)
            def _():
                core_copy(tt, t).start()

        @pl.when(jnp.logical_and(t < last, has_far))
        def _():
            far_copy(tt, t).start()

    own_copy.start()
    own_gust.start()
    send_to(tcount)
    send_to(1)

    for copy in loads:
        copy.wait()

    def turn_coef(tile, first, rows, target):
        cols = pl.ds(pl.multiple_of(tile * STRIP, STRIP), STRIP)
        pair = jnp.concatenate([coef_v[0, :, cols], coef_v[1, :, cols]], axis=0).T
        other = jnp.concatenate([coef_v[2, :, cols], coef_v[2, :, cols]], axis=0).T
        coef_t[0, target : target + rows, :] = pair[first : first + rows]
        coef_t[1, target : target + rows, :] = other[first : first + rows]

    turn_coef(t, 0, STRIP, HALO)

    @pl.when(t > 0)
    def _():
        turn_coef(t - 1, STRIP - HALO, HALO, 0)

    @pl.when(t == 0)
    def _():
        coef_t[0, 0:HALO, :] = zero_halo
        coef_t[1, 0:HALO, :] = zero_halo

    @pl.when(t < last)
    def _():
        turn_coef(t + 1, 0, HALO, HALO + STRIP)

    @pl.when(t == last)
    def _():
        coef_t[0, HALO + STRIP :, :] = zero_halo
        coef_t[1, HALO + STRIP :, :] = zero_halo

    for k in range(2):
        coef_h[k] = pack(coef_t[k, 0:HALF, :], coef_t[k, HALF:, :])

    coef_near.start()

    @pl.when(has_far)
    def _():
        coef_away.start()

    for i in range(2, tcount):
        send_to(i)

    own_copy.wait()

    @pl.when(t < last)
    def _():
        mate_copy(t).start()

    @pl.when(jnp.logical_not(has_far))
    def _():
        coef_far[...] = jnp.zeros_like(coef_far)
        got_far[...] = jnp.zeros_like(got_far)

    mixed = []
    for b in range(KL):
        row = kl_v[0:1, b : b + 1] * cosx_v[0:1, :]
        for a in range(1, KL):
            row = row + kl_v[a : a + 1, b : b + 1] * cosx_v[a : a + 1, :]
        mixed.append(row)
    mixed = jnp.concatenate(mixed + [jnp.zeros((128 - KL, 128), jnp.float32)], axis=0)
    field = jnp.dot(
        cosy_v[...], mixed, precision=lax.Precision.HIGHEST, preferred_element_type=jnp.float32
    )
    stiff[...] = STIFF_SCALE * jnp.exp(0.5 * jnp.tanh(field))

    zero_pad = jnp.zeros((PAD, 128), jnp.float32)
    for buf in (pos, weighted, corr_p, diff_p):
        for i in range(buf.shape[0]):
            buf[i, 0:PAD, :] = zero_pad
            buf[i, PAD + REGION :, :] = zero_pad

    def first_values(own, by_mate, by_far):
        lane = lanes(own.shape[0])
        from_mate = jnp.logical_and(lane >= 64 + 32 * core, lane < 96 + 32 * core)
        return jnp.where(lane < ROWS, own, jnp.where(from_mate, pltpu.roll(by_mate, 64, 1), by_far))

    def second_values(own, by_mate, by_far):
        lane = lanes(own.shape[0])
        from_mate = jnp.logical_and(lane >= 64 + 32 * core, lane < 96 + 32 * core)
        return jnp.where(lane < ROWS, pltpu.roll(own, 64, 1), jnp.where(from_mate, by_mate, by_far))

    def unpack(block, part):
        if part == 0:
            return pltpu.roll(block, 64, 1), block
        right, left = pltpu.roll(block, 32, 1), pltpu.roll(block, 96, 1)
        return jnp.where(core == 1, right, left), jnp.where(core == 1, left, right)

    coef_near.wait_recv()

    @pl.when(has_far)
    def _():
        coef_away.wait_recv()

    for part in range(2):
        for a, b in chunks(0, HALF):
            rows = slice(part * HALF + a, part * HALF + b)
            far_rig, far_mass = unpack(coef_far[0, a:b, :], part)
            far_load, _ = unpack(coef_far[1, a:b, :], part)
            rig = first_values(coef_t[0, rows, :], coef_mate[0, rows, :], far_rig)
            mass = HALF_STEP * second_values(coef_t[0, rows, :], coef_mate[0, rows, :], far_mass)
            stiff[rows, :] *= rig
            kick[0, rows, :] = mass
            kick[1, rows, :] = (1.0 + KEEP) * mass
            kick[2, rows, :] = RATIO * mass
            load[rows, :] = mass * first_values(coef_t[1, rows, :], coef_mate[1, rows, :], far_load)

    def laplace(ref, slot, a, b):
        centre = ref[slot, PAD + a : PAD + b, :]
        rows = ref[slot, PAD + a - 1 : PAD + b - 1, :] + ref[slot, PAD + a + 1 : PAD + b + 1, :]
        sides = pltpu.roll(centre, 1, 1) + pltpu.roll(centre, 127, 1)
        return (rows + sides) - 4.0 * centre

    def stencils(work):
        spans = [chunks(max(lo - 8, 0), min(REGION - lo + 8, REGION)) for _, _, lo, _ in work]
        for k in range(max(map(len, spans))):
            for w, (ref, slot, _, _) in enumerate(work):
                if k < len(spans[w]):
                    a, b = spans[w][k]
                    weighted[w, PAD + a : PAD + b, :] = stiff[a:b, :] * laplace(ref, slot, a, b)
        spans = [chunks(lo, REGION - lo) for _, _, lo, _ in work]
        for k in range(max(map(len, spans))):
            for w, (_, _, _, finish) in enumerate(work):
                if k < len(spans[w]):
                    a, b = spans[w][k]
                    finish(a, b, laplace(weighted, w, a, b))

    def move(slot, g, i):
        push = KEEP * g[i - 1] + g[i]

        def finish(a, b, spring):
            half = (KEEP * KEEP) * vel[slot, a:b, :] - kick[1, a:b, :] * spring + load[a:b, :] * push
            pos[slot, PAD + a : PAD + b, :] += TIME_STEP * half
            vel[slot, a:b, :] = half

        return finish

    def close(slot, g, end):
        def finish(a, b, spring):
            end(
                a,
                b,
                pos[slot, PAD + a : PAD + b, :],
                KEEP * vel[slot, a:b, :] - kick[0, a:b, :] * spring + load[a:b, :] * g[FINE - 1],
            )

        return finish

    def gusts(n):
        return [got_gust[n, i : i + 1, :] for i in range(FINE)]

    def nth(i):
        return lax.rem(t - i + 2 * last, last)

    def forward(n):
        @pl.when(n != t)
        def _():
            core_copy(n, n).wait_recv()
            mate_copy(n).start()

    def receive(slot, n):
        @pl.when(n != t)
        def _():
            gust_copy(n, n).wait_recv()

        @pl.when(has_far)
        def _():
            far_copy(n, n).wait_recv()

        mate_copy(n).wait_recv()
        for part in range(2):
            for a, b in chunks(0, HALF):
                c, d = part * HALF + a, part * HALF + b
                p_far, q_far = unpack(got_far[n, a:b, :], part)
                own = got_core[n, c:d, :]
                other = got_mate[n, c:d, :]
                pos[slot, PAD + c : PAD + d, :] = first_values(own, other, p_far)
                vel[slot, c:d, :] = second_values(own, other, q_far)

    def first_sweep(slices):
        def begin(slot, n, g):
            share = jnp.where(n > 0, 1.0, 0.0)

            def finish(a, b, spring):
                p = pos[slot, PAD + a : PAD + b, :]
                q = vel[slot, a:b, :]
                coarse_q = KEEP_COARSE * q - kick[2, a:b, :] * spring
                diff_q[n, a:b, :] = -share * coarse_q
                diff_p[n, PAD + a : PAD + b, :] = -share * (p + COARSE * coarse_q)
                half = KEEP * q - kick[0, a:b, :] * spring + load[a:b, :] * g[0]
                pos[slot, PAD + a : PAD + b, :] = p + TIME_STEP * half
                vel[slot, a:b, :] = half

            return finish

        def end(n):
            def finish(a, b, new_p, new_q):
                diff_p[n, PAD + a : PAD + b, :] += new_p
                diff_q[n, a:b, :] += new_q

            return finish

        for slot, n in enumerate(slices):
            receive(slot, n)
        todo = [(slot, n, gusts(n)) for slot, n in enumerate(slices)]
        stencils([(pos, slot, 0, begin(slot, n, g)) for slot, n, g in todo])
        for i in range(1, FINE):
            stencils([(pos, slot, 0 if i < 3 else 8, move(slot, g, i)) for slot, n, g in todo])
        stencils([(pos, slot, 8, close(slot, g, end(n))) for slot, n, g in todo])

    own_gust.wait()
    forward(nth(0))
    forward(nth(1))
    forward(nth(2))
    first_sweep([nth(0)])

    def pair(k, carry):
        i = 2 * k + 1

        @pl.when(k < (last - 1) // 2 - 1)
        def _():
            forward(nth(i + 2))
            forward(nth(i + 3))

        first_sweep([nth(i), nth(i + 1)])
        return carry

    lax.fori_loop(0, (last - 1) // 2, pair, 0)

    @pl.when(t != last)
    def _():
        gust_copy(last, last).wait_recv()

    def back_copy(n, slot):
        return remote(outgoing.at[n], incoming.at[slot], back_send.at[n], back_recv.at[slot], n, s)

    def stage(n, a, b, p, q):
        first, end = max(a, HALO), min(b, HALO + STRIP)
        if first < end:
            outgoing[n, first - HALO : end - HALO, :] = jnp.where(
                lanes(end - first) < ROWS,
                p[first - a : end - a],
                pltpu.roll(q[first - a : end - a], 64, 1),
            )

    def send_back(n):
        @pl.when(t != n)
        def _():
            back_copy(n, t).start()

    for a, b in chunks(HALO, HALO + STRIP):
        stage(0, a, b, diff_p[0, PAD + a : PAD + b, :], diff_q[0, a:b, :])
    send_back(0)

    lows = {n: [(10 + 2 * n + 2 * k) // 8 * 8 for k in range(FINE + 1)] for n in range(1, tcount)}

    def begin(n):
        g = gusts(n)

        def finish(a, b, spring):
            p = diff_p[n - 1, PAD + a : PAD + b, :]
            q = diff_q[n - 1, a:b, :]
            if n < last:
                coarse_q = KEEP_COARSE * q - kick[2, a:b, :] * spring
                diff_q[n, a:b, :] += coarse_q
                diff_p[n, PAD + a : PAD + b, :] += p + COARSE * coarse_q
            half = KEEP * q - kick[0, a:b, :] * spring + load[a:b, :] * g[0]
            pos[n, PAD + a : PAD + b, :] = p + TIME_STEP * half
            vel[n, a:b, :] = half

        return finish

    def correct(slot):
        def finish(a, b, spring):
            coarse_q = KEEP_COARSE * corr_q[slot, a:b, :] - kick[2, a:b, :] * spring
            corr_q[slot, a:b, :] = coarse_q
            corr_p[slot, PAD + a : PAD + b, :] += COARSE * coarse_q

        return finish

    def end(n):
        slot = n % 2

        def finish(a, b, new_p, new_q):
            if n > 1:
                new_p = new_p + corr_p[slot, PAD + a : PAD + b, :]
                new_q = new_q + corr_q[slot, a:b, :]
            if n < last:
                corr_p[1 - slot, PAD + a : PAD + b, :] = new_p - diff_p[n, PAD + a : PAD + b, :]
                corr_q[1 - slot, a:b, :] = new_q - diff_q[n, a:b, :]
            stage(n, a, b, new_p, new_q)

        return finish

    for turn in range(1, tcount + FINE):
        work = []
        if turn < tcount:
            work.append((diff_p, turn - 1, lows[turn][0], begin(turn)))
        for i in range(1, FINE):
            n = turn - i
            if 1 <= n < tcount:
                work.append((pos, n, lows[n][i], move(n, gusts(n), i)))
        n = turn - FINE
        if n >= 1:
            if n > 1:
                work.append((corr_p, n % 2, lows[n][FINE], correct(n % 2)))
            work.append((pos, n, lows[n][FINE], close(n, gusts(n), end(n))))
        stencils(work)
        if n >= 1:
            send_back(n)

    def place(tt, block):
        cols = pl.ds(pl.multiple_of(tt * STRIP, STRIP), STRIP)
        out[:, cols] = block.T

    place(t, outgoing[t])
    for i in range(1, tcount):
        tt = lax.rem(t + i, tcount)
        back_copy(tt, tt).wait_recv()
        place(tt, incoming[tt])

    for i in range(1, tcount + 1):
        tt = lax.rem(t + i, tcount)
        if i < tcount:
            back_copy(tt, t).wait_send()
            gust_copy(tt, t).wait_send()

            @pl.when(t < last)
            def _():
                core_copy(tt, t).wait_send()

        @pl.when(tt < last)
        def _():
            mate_copy(tt).wait_send()

        @pl.when(jnp.logical_and(t < last, has_far))
        def _():
            far_copy(tt, t).wait_send()

    coef_near.wait_send()

    @pl.when(has_far)
    def _():
        coef_away.wait_send()


def tables(tcount, scount, rows, cols):
    orders = np.arange(1, KL + 1)
    lane = np.arange(128)
    along = np.where(lane < ROWS + HALO, lane, lane - 128)
    x = np.arange(scount)[:, None] * ROWS + along[None, :]
    y = np.arange(tcount)[:, None] * STRIP - HALO + np.arange(REGION)[None, :]
    cos_x = np.zeros((scount, 8, 128), np.float32)
    cos_x[:, :KL] = np.cos(np.pi * orders[None, :, None] * ((x[:, None, :] + 0.5) / rows))
    cos_y = np.zeros((tcount, REGION, 128), np.float32)
    cos_y[:, :, :KL] = np.cos(np.pi * orders[None, None, :] * ((y[:, :, None] + 0.5) / cols))
    return cos_x, cos_y


def per_device(tcount, scount, start_state, rigidity, inv_mass, gust_load, kl_coeff, gust_history):
    rows, cols = rigidity.shape
    cos_x, cos_y = tables(tcount, scount, rows * scount, cols)
    f32 = jnp.float32
    padded = PAD + REGION + PAD
    packed = (tcount - 1) * STRIP + HALF
    vmem = pltpu.VMEM
    dma = pltpu.SemaphoreType.DMA
    hbm = pl.BlockSpec(memory_space=pltpu.HBM)
    result = pl.pallas_call(
        functools.partial(kernel, tcount, scount),
        out_shape=pltpu.VMEM((2 * rows, cols), f32),
        in_specs=[hbm] * 8,
        out_specs=pl.BlockSpec(memory_space=pltpu.VMEM),
        scratch_shapes=[
            vmem((2 * rows, cols), f32),
            vmem((3, rows, cols), f32),
            vmem((KL, KL), f32),
            vmem((1, FINE), f32),
            vmem((8, 128), f32),
            vmem((REGION, 128), f32),
            vmem((2 * HALO + tcount * STRIP, 128), f32),
            vmem((packed, 128), f32),
            vmem((2, REGION, 128), f32),
            vmem((2, HALF, 128), f32),
            vmem((tcount, REGION, 128), f32),
            vmem((tcount, REGION, 128), f32),
            vmem((tcount, HALF, 128), f32),
            vmem((tcount, 8, 128), f32),
            vmem((2, REGION, 128), f32),
            vmem((2, HALF, 128), f32),
            vmem((8, 128), f32),
            vmem((REGION, 128), f32),
            vmem((3, REGION, 128), f32),
            vmem((REGION, 128), f32),
            vmem((tcount, padded, 128), f32),
            vmem((tcount, REGION, 128), f32),
            vmem((6, padded, 128), f32),
            vmem((tcount - 1, padded, 128), f32),
            vmem((tcount - 1, REGION, 128), f32),
            vmem((2, padded, 128), f32),
            vmem((2, REGION, 128), f32),
            vmem((tcount, STRIP, 128), f32),
            vmem((tcount, STRIP, 128), f32),
            dma((10,)),
            dma((4, tcount)),
            dma((4, tcount)),
            dma((2,)),
            dma((2,)),
            dma((tcount,)),
            dma((tcount,)),
        ],
        compiler_params=pltpu.CompilerParams(
            collective_id=0, has_side_effects=True, vmem_limit_bytes=60 * 1024 * 1024
        ),
    )(
        start_state.reshape(2 * rows, cols),
        rigidity,
        inv_mass,
        gust_load,
        kl_coeff,
        gust_history.reshape(1, FINE),
        jnp.asarray(cos_x),
        jnp.asarray(cos_y),
    )
    return result.reshape(1, 2, rows, cols)


def solution(mesh):
    in_specs = (
        P("tm", None, "space", None),
        P("space", None),
        P("space", None),
        P("space", None),
        P(),
        P("tm"),
    )
    return jax.shard_map(
        functools.partial(per_device, mesh.shape["tm"], mesh.shape["space"]),
        mesh=mesh,
        in_specs=in_specs,
        out_specs=P("tm", None, "space", None),
        check_vma=False,
    )
```

```python
import functools

import jax
import jax.numpy as jnp
import numpy as np
from jax import lax
from jax.experimental import pallas as pl
from jax.experimental.pallas import tpu as pltpu
from jax.sharding import PartitionSpec as P

FINE = 4
KL = 4
STIFF_SCALE = 1.0 / 64.0
TIME_STEP = 0.18
HALF_STEP = 0.09
DAMPING = 0.05
COARSE = FINE * TIME_STEP
KEEP = 1.0 - HALF_STEP * DAMPING
KEEP_COARSE = 1.0 - COARSE * DAMPING
RATIO = COARSE / HALF_STEP

HALO = 32
STRIP = 128
ROWS = 64
REGION = STRIP + 2 * HALO
PAD = 8
HALF = REGION // 2
CHUNK = 32
MESH = pl.DeviceIdType.MESH


def chunks(lo, hi):
    return [(a, min(a + CHUNK, hi)) for a in range(lo, hi, CHUNK)]


def kernel(
    tcount,
    scount,
    state,
    rigidity,
    inv_mass,
    gust_load,
    kl_coeff,
    gust,
    cos_x,
    cos_y,
    out,
    state_v,
    coef_v,
    kl_v,
    gust_v,
    cosx_v,
    cosy_v,
    turned,
    halo,
    coef_t,
    coef_h,
    got_core,
    got_mate,
    got_far,
    got_gust,
    coef_mate,
    coef_far,
    gust_row,
    stiff,
    kick,
    load,
    pos,
    vel,
    weighted,
    diff_p,
    diff_q,
    corr_p,
    corr_q,
    chain_p,
    chain_q,
    closed,
    history,
    kept_p,
    kept_q,
    outgoing,
    incoming,
    local_sem,
    send_sem,
    recv_sem,
    coef_send,
    coef_recv,
    back_send,
    back_recv,
):
    t = lax.axis_index("tm")
    s = lax.axis_index("space")
    last = tcount - 1
    core = lax.rem(s, 2)
    mate = s + 1 - 2 * core
    far = s - 1 + 2 * core
    has_far = jnp.logical_and(far >= 0, far < scount)

    load_state = pltpu.make_async_copy(state, state_v, local_sem.at[0])
    load_state.start()
    load_gust = pltpu.make_async_copy(gust, gust_v, local_sem.at[9])
    load_gust.start()
    loads = [
        pltpu.make_async_copy(src, dst, local_sem.at[1 + i])
        for i, (src, dst) in enumerate(
            [
                (rigidity, coef_v.at[0]),
                (inv_mass, coef_v.at[1]),
                (gust_load, coef_v.at[2]),
                (cos_x.at[s], cosx_v),
                (cos_y.at[t], cosy_v),
                (kl_coeff, kl_v),
            ]
        )
    ]
    for copy in loads:
        copy.start()

    barrier = pltpu.get_barrier_semaphore()

    def greet(tt, ss):
        pl.semaphore_signal(barrier, inc=1, device_id=(tt, ss), device_id_type=MESH)

    for i in range(1, tcount):
        greet(lax.rem(t + i, tcount), s)
    greet(t, mate)

    @pl.when(has_far)
    def _():
        for i in range(tcount):
            greet(lax.rem(t + i, tcount), far)

    def reversed_bits(i):
        return i % 2 * 4 + i // 2 % 2 * 2 + i // 4

    def lanes(rows):
        return lax.broadcasted_iota(jnp.int32, (rows, 128), 1)

    def remote(src, dst, send, recv, tt, ss):
        return pltpu.make_async_remote_copy(
            src_ref=src,
            dst_ref=dst,
            send_sem=send,
            recv_sem=recv,
            device_id=(tt, ss),
            device_id_type=MESH,
        )

    def strip_of(tt, rows):
        return pl.ds(pl.multiple_of(tt * STRIP, STRIP), rows)

    def core_copy(tt, slot):
        return remote(
            turned.at[strip_of(tt, REGION)], got_core.at[slot], send_sem.at[0, tt], recv_sem.at[0, slot], tt, s
        )

    def far_copy(tt, slot):
        return remote(
            halo.at[strip_of(tt, HALF)], got_far.at[slot], send_sem.at[1, tt], recv_sem.at[1, slot], tt, far
        )

    def mate_copy(slot):
        return remote(
            got_core.at[slot], got_mate.at[slot], send_sem.at[2, slot], recv_sem.at[2, slot], t, mate
        )

    def gust_copy(tt, slot):
        return remote(gust_row, got_gust.at[slot], send_sem.at[3, tt], recv_sem.at[3, slot], tt, s)

    coef_near = remote(coef_t, coef_mate, coef_send.at[0], coef_recv.at[0], t, mate)
    coef_away = remote(coef_h, coef_far, coef_send.at[1], coef_recv.at[1], t, far)
    own_copy = pltpu.make_async_copy(turned.at[strip_of(t, REGION)], got_core.at[t], local_sem.at[7])
    own_gust = pltpu.make_async_copy(gust_row, got_gust.at[t], local_sem.at[8])

    zero_halo = jnp.zeros((HALO, 128), jnp.float32)
    turned[0:HALO, :] = zero_halo
    turned[HALO + tcount * STRIP :, :] = zero_halo
    load_state.wait()
    load_gust.wait()
    for i in range(tcount):
        turned[HALO + i * STRIP : HALO + (i + 1) * STRIP, :] = state_v[
            :, i * STRIP : (i + 1) * STRIP
        ].T
    row8 = lax.broadcasted_iota(jnp.int32, (8, 128), 0)
    gust_block = jnp.zeros((8, 128), jnp.float32)
    for i in range(FINE):
        gust_block = jnp.where(row8 == i, gust_v[0:1, i : i + 1], gust_block)
    gust_row[...] = gust_block

    def pack(near, further):
        upper = lax.rem(lanes(near.shape[0]), 64) >= 32
        return jnp.where(
            core == 0,
            jnp.where(upper, pltpu.roll(further, 32, 1), near),
            jnp.where(upper, near, pltpu.roll(further, 96, 1)),
        )

    for a, b in chunks(0, halo.shape[0]):
        halo[a:b, :] = pack(turned[a:b, :], turned[HALF + a : HALF + b, :])

    pl.semaphore_wait(barrier, tcount + tcount * has_far.astype(jnp.int32))

    def send_to(i):
        tt = lax.rem(t + reversed_bits(i), tcount)
        if i > 0:
            gust_copy(tt, t).start()

            @pl.when(t < last)
            def _():
                core_copy(tt, t).start()

        @pl.when(jnp.logical_and(t < last, has_far))
        def _():
            far_copy(tt, t).start()

    own_copy.start()
    own_gust.start()
    send_to(0)
    send_to(1)

    for copy in loads:
        copy.wait()

    def turn_coef(tile, first, rows, target):
        cols = pl.ds(pl.multiple_of(tile * STRIP, STRIP), STRIP)
        pair = jnp.concatenate([coef_v[0, :, cols], coef_v[1, :, cols]], axis=0).T
        other = jnp.concatenate([coef_v[2, :, cols], coef_v[2, :, cols]], axis=0).T
        coef_t[0, target : target + rows, :] = pair[first : first + rows]
        coef_t[1, target : target + rows, :] = other[first : first + rows]

    turn_coef(t, 0, STRIP, HALO)

    @pl.when(t > 0)
    def _():
        turn_coef(t - 1, STRIP - HALO, HALO, 0)

    @pl.when(t == 0)
    def _():
        coef_t[0, 0:HALO, :] = zero_halo
        coef_t[1, 0:HALO, :] = zero_halo

    @pl.when(t < last)
    def _():
        turn_coef(t + 1, 0, HALO, HALO + STRIP)

    @pl.when(t == last)
    def _():
        coef_t[0, HALO + STRIP :, :] = zero_halo
        coef_t[1, HALO + STRIP :, :] = zero_halo

    for k in range(2):
        coef_h[k] = pack(coef_t[k, 0:HALF, :], coef_t[k, HALF:, :])

    coef_near.start()

    @pl.when(has_far)
    def _():
        coef_away.start()

    for i in range(2, tcount):
        send_to(i)

    own_copy.wait()

    @pl.when(t < last)
    def _():
        mate_copy(t).start()

    @pl.when(jnp.logical_not(has_far))
    def _():
        coef_far[...] = jnp.zeros_like(coef_far)
        got_far[...] = jnp.zeros_like(got_far)

    mixed = []
    for b in range(KL):
        row = kl_v[0:1, b : b + 1] * cosx_v[0:1, :]
        for a in range(1, KL):
            row = row + kl_v[a : a + 1, b : b + 1] * cosx_v[a : a + 1, :]
        mixed.append(row)
    mixed = jnp.concatenate(mixed + [jnp.zeros((128 - KL, 128), jnp.float32)], axis=0)
    field = jnp.dot(
        cosy_v[...], mixed, precision=lax.Precision.HIGHEST, preferred_element_type=jnp.float32
    )
    stiff[...] = STIFF_SCALE * jnp.exp(0.5 * jnp.tanh(field))

    zero_pad = jnp.zeros((PAD, 128), jnp.float32)
    for buf in (pos, weighted, corr_p, diff_p):
        for i in range(buf.shape[0]):
            buf[i, 0:PAD, :] = zero_pad
            buf[i, PAD + REGION :, :] = zero_pad

    def first_values(own, by_mate, by_far):
        lane = lanes(own.shape[0])
        from_mate = jnp.logical_and(lane >= 64 + 32 * core, lane < 96 + 32 * core)
        return jnp.where(lane < ROWS, own, jnp.where(from_mate, pltpu.roll(by_mate, 64, 1), by_far))

    def second_values(own, by_mate, by_far):
        lane = lanes(own.shape[0])
        from_mate = jnp.logical_and(lane >= 64 + 32 * core, lane < 96 + 32 * core)
        return jnp.where(lane < ROWS, pltpu.roll(own, 64, 1), jnp.where(from_mate, by_mate, by_far))

    def unpack(block, part):
        if part == 0:
            return pltpu.roll(block, 64, 1), block
        right, left = pltpu.roll(block, 32, 1), pltpu.roll(block, 96, 1)
        return jnp.where(core == 1, right, left), jnp.where(core == 1, left, right)

    coef_near.wait_recv()

    @pl.when(has_far)
    def _():
        coef_away.wait_recv()

    for part in range(2):
        for a, b in chunks(0, HALF):
            rows = slice(part * HALF + a, part * HALF + b)
            far_rig, far_mass = unpack(coef_far[0, a:b, :], part)
            far_load, _ = unpack(coef_far[1, a:b, :], part)
            rig = first_values(coef_t[0, rows, :], coef_mate[0, rows, :], far_rig)
            mass = HALF_STEP * second_values(coef_t[0, rows, :], coef_mate[0, rows, :], far_mass)
            stiff[rows, :] *= rig
            kick[0, rows, :] = mass
            kick[1, rows, :] = (1.0 + KEEP) * mass
            kick[2, rows, :] = RATIO * mass
            load[rows, :] = mass * first_values(coef_t[1, rows, :], coef_mate[1, rows, :], far_load)

    def laplace(ref, slot, a, b):
        centre = ref[slot, PAD + a : PAD + b, :]
        rows = ref[slot, PAD + a - 1 : PAD + b - 1, :] + ref[slot, PAD + a + 1 : PAD + b + 1, :]
        sides = pltpu.roll(centre, 1, 1) + pltpu.roll(centre, 127, 1)
        return (rows + sides) - 4.0 * centre

    def stencils(work):
        spans = [chunks(max(lo - 8, 0), min(REGION - lo + 8, REGION)) for _, _, lo, _ in work]
        for k in range(max(map(len, spans))):
            for w, (ref, slot, _, _) in enumerate(work):
                if k < len(spans[w]):
                    a, b = spans[w][k]
                    weighted[w, PAD + a : PAD + b, :] = stiff[a:b, :] * laplace(ref, slot, a, b)
        spans = [chunks(lo, REGION - lo) for _, _, lo, _ in work]
        for k in range(max(map(len, spans))):
            for w, (_, _, _, finish) in enumerate(work):
                if k < len(spans[w]):
                    a, b = spans[w][k]
                    finish(a, b, laplace(weighted, w, a, b))

    def move(slot, target, g, i):
        push = KEEP * g[i - 1] + g[i]

        def finish(a, b, spring):
            half = (KEEP * KEEP) * vel[slot, a:b, :] - kick[1, a:b, :] * spring + load[a:b, :] * push
            pos[target, PAD + a : PAD + b, :] = pos[slot, PAD + a : PAD + b, :] + TIME_STEP * half
            vel[target, a:b, :] = half

        return finish

    def close(slot, g, end):
        def finish(a, b, spring):
            end(
                a,
                b,
                pos[slot, PAD + a : PAD + b, :],
                KEEP * vel[slot, a:b, :] - kick[0, a:b, :] * spring + load[a:b, :] * g[FINE - 1],
            )

        return finish

    def gusts(n):
        return [got_gust[n, i : i + 1, :] for i in range(FINE)]

    def nth(i):
        skipped = reversed_bits(lax.rem(t + 1, tcount))
        place_in_order = i + jnp.where(i >= skipped, 1, 0)
        return lax.rem(t - reversed_bits(place_in_order) + tcount, tcount)

    def forward(n):
        @pl.when(n != t)
        def _():
            core_copy(n, n).wait_recv()
            mate_copy(n).start()

    def receive(slot, n):
        @pl.when(n != t)
        def _():
            gust_copy(n, n).wait_recv()

        @pl.when(has_far)
        def _():
            far_copy(n, n).wait_recv()

        mate_copy(n).wait_recv()
        for part in range(2):
            for a, b in chunks(0, HALF):
                c, d = part * HALF + a, part * HALF + b
                p_far, q_far = unpack(got_far[n, a:b, :], part)
                own = got_core[n, c:d, :]
                other = got_mate[n, c:d, :]
                pos[slot, PAD + c : PAD + d, :] = first_values(own, other, p_far)
                vel[slot, c:d, :] = second_values(own, other, q_far)

    def first_sweep(slices):
        def begin(slot, n, g):
            share = jnp.where(n > 0, 1.0, 0.0)

            def finish(a, b, spring):
                p = pos[slot, PAD + a : PAD + b, :]
                q = vel[slot, a:b, :]
                coarse_q = KEEP_COARSE * q - kick[2, a:b, :] * spring
                kept_q[slot, a:b, :] = -share * coarse_q
                kept_p[slot, a:b, :] = -share * (p + COARSE * coarse_q)
                half = KEEP * q - kick[0, a:b, :] * spring + load[a:b, :] * g[0]
                pos[slot, PAD + a : PAD + b, :] = p + TIME_STEP * half
                vel[slot, a:b, :] = half

            return finish

        def end(slot):
            def finish(a, b, new_p, new_q):
                kept_p[slot, a:b, :] += new_p
                kept_q[slot, a:b, :] += new_q

            return finish

        for slot, n in enumerate(slices):
            receive(slot, n)
        todo = [(slot, n, gusts(n)) for slot, n in enumerate(slices)]
        stencils([(pos, slot, 0, begin(slot, n, g)) for slot, n, g in todo])
        for i in range(1, FINE):
            stencils([(pos, slot, 0 if i < 3 else 8, move(slot, slot, g, i)) for slot, n, g in todo])
        stencils([(pos, slot, 8, close(slot, g, end(slot))) for slot, n, g in todo])
        for slot, n, _ in todo:
            diff_p[n, PAD : PAD + REGION, :] = kept_p[slot]
            diff_q[n] = kept_q[slot]

    own_gust.wait()
    forward(nth(0))
    first_sweep([nth(0)])
    forward(nth(1))
    forward(nth(2))

    def pair(k, carry):
        i = 2 * k + 1

        @pl.when(k == 1)
        def _():
            for later in range(3, last):
                forward(nth(later))

        first_sweep([nth(i), nth(i + 1)])
        return carry

    lax.fori_loop(0, (last - 1) // 2, pair, 0)

    @pl.when(t != last)
    def _():
        gust_copy(last, last).wait_recv()

    def back_copy(n, slot):
        return remote(outgoing.at[n], incoming.at[slot], back_send.at[n], back_recv.at[slot], n, s)

    def stage(n, a, b, p, q):
        first, end = max(a, HALO), min(b, HALO + STRIP)
        if first < end:
            outgoing[n, first - HALO : end - HALO, :] = jnp.where(
                lanes(end - first) < ROWS,
                p[first - a : end - a],
                pltpu.roll(q[first - a : end - a], 64, 1),
            )

    def send_back(n):
        @pl.when(t != n)
        def _():
            back_copy(n, t).start()

    for a, b in chunks(HALO, HALO + STRIP):
        stage(0, a, b, diff_p[0, PAD + a : PAD + b, :], diff_q[0, a:b, :])
    send_back(0)

    def begin(k):
        g = gusts(k)

        def finish(a, b, spring):
            p = chain_p[0, PAD + a : PAD + b, :]
            q = chain_q[a:b, :]
            coarse_q = KEEP_COARSE * q - kick[2, a:b, :] * spring
            next_q = diff_q[k, a:b, :] + coarse_q
            next_p = diff_p[k, PAD + a : PAD + b, :] + (p + COARSE * coarse_q)
            chain_q[a:b, :] = next_q
            chain_p[0, PAD + a : PAD + b, :] = next_p
            half = KEEP * q - kick[0, a:b, :] * spring + load[a:b, :] * g[0]
            pos[0, PAD + a : PAD + b, :] = p + TIME_STEP * half
            vel[0, a:b, :] = half

        return finish

    def correct(a, b, spring):
        coarse_q = KEEP_COARSE * corr_q[a:b, :] - kick[2, a:b, :] * spring
        corr_q[a:b, :] = coarse_q
        corr_p[0, PAD + a : PAD + b, :] += COARSE * coarse_q

    def end(n):
        def finish(a, b, new_p, new_q):
            new_p = new_p + corr_p[0, PAD + a : PAD + b, :]
            new_q = new_q + corr_q[a:b, :]
            corr_p[0, PAD + a : PAD + b, :] = new_p - history[n, 0, a:b, :]
            corr_q[a:b, :] = new_q - history[n, 1, a:b, :]
            closed[0, a:b, :] = new_p
            closed[1, a:b, :] = new_q

        return finish

    def turn(k, lo, stages):
        work = []
        if FINE in stages:
            n = k - FINE
            work.append((corr_p, 0, lo, correct))
            work.append((pos, FINE - 1, lo, close(FINE - 1, gusts(n), end(n))))
        for i in reversed(range(1, FINE)):
            if i in stages:
                work.append((pos, i - 1, lo, move(i - 1, i, gusts(lax.rem(k - i + tcount, tcount)), i)))
        if 0 in stages:
            work.append((chain_p, 0, lo, begin(k)))
        stencils(work)
        if 0 in stages:
            history[k, 0, lo : REGION - lo, :] = chain_p[0, PAD + lo : PAD + REGION - lo, :]
            history[k, 1, lo : REGION - lo, :] = chain_q[lo : REGION - lo, :]
        if FINE in stages:
            stage(k - FINE, HALO, HALO + STRIP, closed[0, HALO : HALO + STRIP, :], closed[1, HALO : HALO + STRIP, :])
            send_back(k - FINE)

    def turns(first, end_turn, stages):
        def step(k, carry):
            turn(k, (10 + 2 * first) // 8 * 8, stages)
            return carry

        lax.fori_loop(first, end_turn, step, 0)

    chain_p[...] = diff_p[0:1]
    chain_q[...] = diff_q[0]
    corr_p[...] = jnp.zeros_like(corr_p)
    corr_q[...] = jnp.zeros_like(corr_q)
    for k in range(1, FINE + 1):
        turn(k, (10 + 2 * k) // 8 * 8, range(k))
    turns(FINE + 1, tcount, range(FINE + 1))
    for k in range(tcount, tcount + FINE):
        turn(k, (10 + 2 * k) // 8 * 8, range(k - tcount + 1, FINE + 1))

    def place(tt, block):
        cols = pl.ds(pl.multiple_of(tt * STRIP, STRIP), STRIP)
        out[:, cols] = block.T

    place(t, outgoing[t])
    for i in range(1, tcount):
        tt = lax.rem(t + i, tcount)
        back_copy(tt, tt).wait_recv()
        place(tt, incoming[tt])

    for i in range(1, tcount + 1):
        tt = lax.rem(t + i, tcount)
        if i < tcount:
            back_copy(tt, t).wait_send()
            gust_copy(tt, t).wait_send()

            @pl.when(t < last)
            def _():
                core_copy(tt, t).wait_send()

        @pl.when(tt < last)
        def _():
            mate_copy(tt).wait_send()

        @pl.when(jnp.logical_and(t < last, has_far))
        def _():
            far_copy(tt, t).wait_send()

    coef_near.wait_send()

    @pl.when(has_far)
    def _():
        coef_away.wait_send()


def tables(tcount, scount, rows, cols):
    orders = np.arange(1, KL + 1)
    lane = np.arange(128)
    along = np.where(lane < ROWS + HALO, lane, lane - 128)
    x = np.arange(scount)[:, None] * ROWS + along[None, :]
    y = np.arange(tcount)[:, None] * STRIP - HALO + np.arange(REGION)[None, :]
    cos_x = np.zeros((scount, 8, 128), np.float32)
    cos_x[:, :KL] = np.cos(np.pi * orders[None, :, None] * ((x[:, None, :] + 0.5) / rows))
    cos_y = np.zeros((tcount, REGION, 128), np.float32)
    cos_y[:, :, :KL] = np.cos(np.pi * orders[None, None, :] * ((y[:, :, None] + 0.5) / cols))
    return cos_x, cos_y


def per_device(tcount, scount, start_state, rigidity, inv_mass, gust_load, kl_coeff, gust_history):
    rows, cols = rigidity.shape
    cos_x, cos_y = tables(tcount, scount, rows * scount, cols)
    f32 = jnp.float32
    padded = PAD + REGION + PAD
    packed = (tcount - 1) * STRIP + HALF
    vmem = pltpu.VMEM
    dma = pltpu.SemaphoreType.DMA
    hbm = pl.BlockSpec(memory_space=pltpu.HBM)
    result = pl.pallas_call(
        functools.partial(kernel, tcount, scount),
        out_shape=pltpu.VMEM((2 * rows, cols), f32),
        in_specs=[hbm] * 8,
        out_specs=pl.BlockSpec(memory_space=pltpu.VMEM),
        scratch_shapes=[
            vmem((2 * rows, cols), f32),
            vmem((3, rows, cols), f32),
            vmem((KL, KL), f32),
            vmem((1, FINE), f32),
            vmem((8, 128), f32),
            vmem((REGION, 128), f32),
            vmem((2 * HALO + tcount * STRIP, 128), f32),
            vmem((packed, 128), f32),
            vmem((2, REGION, 128), f32),
            vmem((2, HALF, 128), f32),
            vmem((tcount, REGION, 128), f32),
            vmem((tcount, REGION, 128), f32),
            vmem((tcount, HALF, 128), f32),
            vmem((tcount, 8, 128), f32),
            vmem((2, REGION, 128), f32),
            vmem((2, HALF, 128), f32),
            vmem((8, 128), f32),
            vmem((REGION, 128), f32),
            vmem((3, REGION, 128), f32),
            vmem((REGION, 128), f32),
            vmem((FINE, padded, 128), f32),
            vmem((FINE, REGION, 128), f32),
            vmem((6, padded, 128), f32),
            vmem((tcount, padded, 128), f32),
            vmem((tcount, REGION, 128), f32),
            vmem((1, padded, 128), f32),
            vmem((REGION, 128), f32),
            vmem((1, padded, 128), f32),
            vmem((REGION, 128), f32),
            vmem((2, REGION, 128), f32),
            vmem((tcount, 2, REGION, 128), f32),
            vmem((2, REGION, 128), f32),
            vmem((2, REGION, 128), f32),
            vmem((tcount, STRIP, 128), f32),
            vmem((tcount, STRIP, 128), f32),
            dma((10,)),
            dma((4, tcount)),
            dma((4, tcount)),
            dma((2,)),
            dma((2,)),
            dma((tcount,)),
            dma((tcount,)),
        ],
        compiler_params=pltpu.CompilerParams(
            collective_id=0, has_side_effects=True, vmem_limit_bytes=60 * 1024 * 1024
        ),
    )(
        start_state.reshape(2 * rows, cols),
        rigidity,
        inv_mass,
        gust_load,
        kl_coeff,
        gust_history.reshape(1, FINE),
        jnp.asarray(cos_x),
        jnp.asarray(cos_y),
    )
    return result.reshape(1, 2, rows, cols)


def solution(mesh):
    in_specs = (
        P("tm", None, "space", None),
        P("space", None),
        P("space", None),
        P("space", None),
        P(),
        P("tm"),
    )
    return jax.shard_map(
        functools.partial(per_device, mesh.shape["tm"], mesh.shape["space"]),
        mesh=mesh,
        in_specs=in_specs,
        out_specs=P("tm", None, "space", None),
        check_vma=False,
    )
```

```python
import functools

import jax
import jax.numpy as jnp
import numpy as np
from jax import lax
from jax.experimental import pallas as pl
from jax.experimental.pallas import tpu as pltpu
from jax.sharding import PartitionSpec as P

FINE = 4
KL = 4
STIFF_SCALE = 1.0 / 64.0
TIME_STEP = 0.18
HALF_STEP = 0.09
DAMPING = 0.05
COARSE = FINE * TIME_STEP
KEEP = 1.0 - HALF_STEP * DAMPING
KEEP_COARSE = 1.0 - COARSE * DAMPING
RATIO = COARSE / HALF_STEP

HALO = 32
STRIP = 128
ROWS = 64
REGION = STRIP + 2 * HALO
PAD = 8
HALF = REGION // 2
CHUNK = 32
MESH = pl.DeviceIdType.MESH


def chunks(lo, hi):
    return [(a, min(a + CHUNK, hi)) for a in range(lo, hi, CHUNK)]


def kernel(
    tcount,
    scount,
    state,
    rigidity,
    inv_mass,
    gust_load,
    kl_coeff,
    gust,
    cos_x,
    cos_y,
    out,
    state_v,
    coef_v,
    kl_v,
    gust_v,
    cosx_v,
    cosy_v,
    turned,
    halo,
    coef_t,
    coef_h,
    got_core,
    got_mate,
    got_far,
    got_gust,
    coef_mate,
    coef_far,
    gust_row,
    stiff,
    kick,
    load,
    pos,
    vel,
    weighted,
    diff_p,
    diff_q,
    corr_p,
    corr_q,
    chain_p,
    chain_q,
    closed,
    history,
    kept_p,
    kept_q,
    outgoing,
    incoming,
    local_sem,
    send_sem,
    recv_sem,
    coef_send,
    coef_recv,
    back_send,
    back_recv,
):
    t = lax.axis_index("tm")
    s = lax.axis_index("space")
    last = tcount - 1
    core = lax.rem(s, 2)
    mate = s + 1 - 2 * core
    far = s - 1 + 2 * core
    has_far = jnp.logical_and(far >= 0, far < scount)

    load_state = pltpu.make_async_copy(state, state_v, local_sem.at[0])
    load_state.start()
    load_gust = pltpu.make_async_copy(gust, gust_v, local_sem.at[9])
    load_gust.start()
    loads = [
        pltpu.make_async_copy(src, dst, local_sem.at[1 + i])
        for i, (src, dst) in enumerate(
            [
                (rigidity, coef_v.at[0]),
                (inv_mass, coef_v.at[1]),
                (gust_load, coef_v.at[2]),
                (cos_x.at[s], cosx_v),
                (cos_y.at[t], cosy_v),
                (kl_coeff, kl_v),
            ]
        )
    ]
    for copy in loads:
        copy.start()

    barrier = pltpu.get_barrier_semaphore()

    def greet(tt, ss):
        pl.semaphore_signal(barrier, inc=1, device_id=(tt, ss), device_id_type=MESH)

    for i in range(1, tcount):
        greet(lax.rem(t + i, tcount), s)
    greet(t, mate)

    @pl.when(has_far)
    def _():
        for i in range(tcount):
            greet(lax.rem(t + i, tcount), far)

    def reversed_bits(i):
        return i % 2 * 4 + i // 2 % 2 * 2 + i // 4

    def lanes(rows):
        return lax.broadcasted_iota(jnp.int32, (rows, 128), 1)

    def remote(src, dst, send, recv, tt, ss):
        return pltpu.make_async_remote_copy(
            src_ref=src,
            dst_ref=dst,
            send_sem=send,
            recv_sem=recv,
            device_id=(tt, ss),
            device_id_type=MESH,
        )

    def strip_of(tt, rows):
        return pl.ds(pl.multiple_of(tt * STRIP, STRIP), rows)

    def core_copy(tt, slot):
        return remote(
            turned.at[strip_of(tt, REGION)], got_core.at[slot], send_sem.at[0, tt], recv_sem.at[0, slot], tt, s
        )

    def far_copy(tt, slot):
        return remote(
            halo.at[strip_of(tt, HALF)], got_far.at[slot], send_sem.at[1, tt], recv_sem.at[1, slot], tt, far
        )

    def mate_copy(slot):
        return remote(
            got_core.at[slot], got_mate.at[slot], send_sem.at[2, slot], recv_sem.at[2, slot], t, mate
        )

    def gust_copy(tt, slot):
        return remote(gust_row, got_gust.at[slot], send_sem.at[3, tt], recv_sem.at[3, slot], tt, s)

    coef_near = remote(coef_t, coef_mate, coef_send.at[0], coef_recv.at[0], t, mate)
    coef_away = remote(coef_h, coef_far, coef_send.at[1], coef_recv.at[1], t, far)
    own_copy = pltpu.make_async_copy(turned.at[strip_of(t, REGION)], got_core.at[t], local_sem.at[7])
    own_gust = pltpu.make_async_copy(gust_row, got_gust.at[t], local_sem.at[8])

    zero_halo = jnp.zeros((HALO, 128), jnp.float32)
    turned[0:HALO, :] = zero_halo
    turned[HALO + tcount * STRIP :, :] = zero_halo
    load_state.wait()
    load_gust.wait()
    for i in range(tcount):
        turned[HALO + i * STRIP : HALO + (i + 1) * STRIP, :] = state_v[
            :, i * STRIP : (i + 1) * STRIP
        ].T
    row8 = lax.broadcasted_iota(jnp.int32, (8, 128), 0)
    gust_block = jnp.zeros((8, 128), jnp.float32)
    for i in range(FINE):
        gust_block = jnp.where(row8 == i, gust_v[0:1, i : i + 1], gust_block)
    gust_row[...] = gust_block

    def pack(near, further):
        upper = lax.rem(lanes(near.shape[0]), 64) >= 32
        return jnp.where(
            core == 0,
            jnp.where(upper, pltpu.roll(further, 32, 1), near),
            jnp.where(upper, near, pltpu.roll(further, 96, 1)),
        )

    pl.semaphore_wait(barrier, tcount + tcount * has_far.astype(jnp.int32))

    def send_core(i):
        tt = lax.rem(t + reversed_bits(i), tcount)
        gust_copy(tt, t).start()

        @pl.when(t < last)
        def _():
            core_copy(tt, t).start()

    def send_far(i):
        tt = lax.rem(t + reversed_bits(i), tcount)

        @pl.when(jnp.logical_and(t < last, has_far))
        def _():
            far_copy(tt, t).start()

    own_copy.start()
    own_gust.start()
    for i in range(1, 4):
        send_core(i)
    for a, b in chunks(0, halo.shape[0]):
        halo[a:b, :] = pack(turned[a:b, :], turned[HALF + a : HALF + b, :])

    send_far(0)
    send_far(1)

    for copy in loads:
        copy.wait()

    def turn_coef(tile, first, rows, target):
        cols = pl.ds(pl.multiple_of(tile * STRIP, STRIP), STRIP)
        pair = jnp.concatenate([coef_v[0, :, cols], coef_v[1, :, cols]], axis=0).T
        other = jnp.concatenate([coef_v[2, :, cols], coef_v[2, :, cols]], axis=0).T
        coef_t[0, target : target + rows, :] = pair[first : first + rows]
        coef_t[1, target : target + rows, :] = other[first : first + rows]

    turn_coef(t, 0, STRIP, HALO)

    @pl.when(t > 0)
    def _():
        turn_coef(t - 1, STRIP - HALO, HALO, 0)

    @pl.when(t == 0)
    def _():
        coef_t[0, 0:HALO, :] = zero_halo
        coef_t[1, 0:HALO, :] = zero_halo

    @pl.when(t < last)
    def _():
        turn_coef(t + 1, 0, HALO, HALO + STRIP)

    @pl.when(t == last)
    def _():
        coef_t[0, HALO + STRIP :, :] = zero_halo
        coef_t[1, HALO + STRIP :, :] = zero_halo

    for k in range(2):
        coef_h[k] = pack(coef_t[k, 0:HALF, :], coef_t[k, HALF:, :])

    coef_near.start()

    @pl.when(has_far)
    def _():
        coef_away.start()

    for i in range(2, tcount):
        if i >= 4:
            send_core(i)
        send_far(i)

    own_copy.wait()

    @pl.when(t < last)
    def _():
        mate_copy(t).start()

    @pl.when(jnp.logical_not(has_far))
    def _():
        coef_far[...] = jnp.zeros_like(coef_far)
        got_far[...] = jnp.zeros_like(got_far)

    mixed = []
    for b in range(KL):
        row = kl_v[0:1, b : b + 1] * cosx_v[0:1, :]
        for a in range(1, KL):
            row = row + kl_v[a : a + 1, b : b + 1] * cosx_v[a : a + 1, :]
        mixed.append(row)
    mixed = jnp.concatenate(mixed + [jnp.zeros((128 - KL, 128), jnp.float32)], axis=0)
    field = jnp.dot(
        cosy_v[...], mixed, precision=lax.Precision.HIGHEST, preferred_element_type=jnp.float32
    )
    stiff[...] = STIFF_SCALE * jnp.exp(0.5 * jnp.tanh(field))

    zero_pad = jnp.zeros((PAD, 128), jnp.float32)
    for buf in (pos, weighted, corr_p, diff_p):
        for i in range(buf.shape[0]):
            buf[i, 0:PAD, :] = zero_pad
            buf[i, PAD + REGION :, :] = zero_pad

    def first_values(own, by_mate, by_far):
        lane = lanes(own.shape[0])
        from_mate = jnp.logical_and(lane >= 64 + 32 * core, lane < 96 + 32 * core)
        return jnp.where(lane < ROWS, own, jnp.where(from_mate, pltpu.roll(by_mate, 64, 1), by_far))

    def second_values(own, by_mate, by_far):
        lane = lanes(own.shape[0])
        from_mate = jnp.logical_and(lane >= 64 + 32 * core, lane < 96 + 32 * core)
        return jnp.where(lane < ROWS, pltpu.roll(own, 64, 1), jnp.where(from_mate, by_mate, by_far))

    def unpack(block, part):
        if part == 0:
            return pltpu.roll(block, 64, 1), block
        right, left = pltpu.roll(block, 32, 1), pltpu.roll(block, 96, 1)
        return jnp.where(core == 1, right, left), jnp.where(core == 1, left, right)

    coef_near.wait_recv()

    @pl.when(has_far)
    def _():
        coef_away.wait_recv()

    for part in range(2):
        for a, b in chunks(0, HALF):
            rows = slice(part * HALF + a, part * HALF + b)
            far_rig, far_mass = unpack(coef_far[0, a:b, :], part)
            far_load, _ = unpack(coef_far[1, a:b, :], part)
            rig = first_values(coef_t[0, rows, :], coef_mate[0, rows, :], far_rig)
            mass = HALF_STEP * second_values(coef_t[0, rows, :], coef_mate[0, rows, :], far_mass)
            stiff[rows, :] *= rig
            kick[0, rows, :] = mass
            kick[1, rows, :] = (1.0 + KEEP) * mass
            kick[2, rows, :] = RATIO * mass
            load[rows, :] = mass * first_values(coef_t[1, rows, :], coef_mate[1, rows, :], far_load)

    def laplace(ref, slot, a, b):
        centre = ref[slot, PAD + a : PAD + b, :]
        rows = ref[slot, PAD + a - 1 : PAD + b - 1, :] + ref[slot, PAD + a + 1 : PAD + b + 1, :]
        sides = pltpu.roll(centre, 1, 1) + pltpu.roll(centre, 127, 1)
        return (rows + sides) - 4.0 * centre

    def stencils(work):
        spans = [chunks(max(lo - 8, 0), min(REGION - lo + 8, REGION)) for _, _, lo, _ in work]
        for k in range(max(map(len, spans))):
            for w, (ref, slot, _, _) in enumerate(work):
                if k < len(spans[w]):
                    a, b = spans[w][k]
                    weighted[w, PAD + a : PAD + b, :] = stiff[a:b, :] * laplace(ref, slot, a, b)
        spans = [chunks(lo, REGION - lo) for _, _, lo, _ in work]
        for k in range(max(map(len, spans))):
            for w, (_, _, _, finish) in enumerate(work):
                if k < len(spans[w]):
                    a, b = spans[w][k]
                    finish(a, b, laplace(weighted, w, a, b))

    def move(slot, target, g, i):
        push = KEEP * g[i - 1] + g[i]

        def finish(a, b, spring):
            half = (KEEP * KEEP) * vel[slot, a:b, :] - kick[1, a:b, :] * spring + load[a:b, :] * push
            pos[target, PAD + a : PAD + b, :] = pos[slot, PAD + a : PAD + b, :] + TIME_STEP * half
            vel[target, a:b, :] = half

        return finish

    def close(slot, g, end):
        def finish(a, b, spring):
            end(
                a,
                b,
                pos[slot, PAD + a : PAD + b, :],
                KEEP * vel[slot, a:b, :] - kick[0, a:b, :] * spring + load[a:b, :] * g[FINE - 1],
            )

        return finish

    def gusts(n):
        return [got_gust[n, i : i + 1, :] for i in range(FINE)]

    def nth(i):
        skipped = reversed_bits(lax.rem(t + 1, tcount))
        place_in_order = i + jnp.where(i >= skipped, 1, 0)
        return lax.rem(t - reversed_bits(place_in_order) + tcount, tcount)

    def forward(n):
        @pl.when(n != t)
        def _():
            core_copy(n, n).wait_recv()
            mate_copy(n).start()

    def receive(slot, n):
        @pl.when(n != t)
        def _():
            gust_copy(n, n).wait_recv()

        @pl.when(has_far)
        def _():
            far_copy(n, n).wait_recv()

        mate_copy(n).wait_recv()
        for part in range(2):
            for a, b in chunks(0, HALF):
                c, d = part * HALF + a, part * HALF + b
                p_far, q_far = unpack(got_far[n, a:b, :], part)
                own = got_core[n, c:d, :]
                other = got_mate[n, c:d, :]
                pos[slot, PAD + c : PAD + d, :] = first_values(own, other, p_far)
                vel[slot, c:d, :] = second_values(own, other, q_far)

    def first_sweep(slices):
        def begin(slot, n, g):
            share = jnp.where(n > 0, 1.0, 0.0)

            def finish(a, b, spring):
                p = pos[slot, PAD + a : PAD + b, :]
                q = vel[slot, a:b, :]
                coarse_q = KEEP_COARSE * q - kick[2, a:b, :] * spring
                kept_q[slot, a:b, :] = -share * coarse_q
                kept_p[slot, a:b, :] = -share * (p + COARSE * coarse_q)
                half = KEEP * q - kick[0, a:b, :] * spring + load[a:b, :] * g[0]
                pos[slot, PAD + a : PAD + b, :] = p + TIME_STEP * half
                vel[slot, a:b, :] = half

            return finish

        def end(slot):
            def finish(a, b, new_p, new_q):
                kept_p[slot, a:b, :] += new_p
                kept_q[slot, a:b, :] += new_q

            return finish

        for slot, n in enumerate(slices):
            receive(slot, n)
        todo = [(slot, n, gusts(n)) for slot, n in enumerate(slices)]
        stencils([(pos, slot, 0, begin(slot, n, g)) for slot, n, g in todo])
        for i in range(1, FINE):
            stencils([(pos, slot, 0 if i < 3 else 8, move(slot, slot, g, i)) for slot, n, g in todo])
        stencils([(pos, slot, 8, close(slot, g, end(slot))) for slot, n, g in todo])
        for slot, n, _ in todo:
            diff_p[n, PAD : PAD + REGION, :] = kept_p[slot]
            diff_q[n] = kept_q[slot]

    own_gust.wait()
    forward(nth(0))
    first_sweep([nth(0)])
    forward(nth(1))
    forward(nth(2))

    def pair(k, carry):
        i = 2 * k + 1

        @pl.when(k == 1)
        def _():
            for later in range(3, last):
                forward(nth(later))

        first_sweep([nth(i), nth(i + 1)])
        return carry

    lax.fori_loop(0, (last - 1) // 2, pair, 0)

    @pl.when(t != last)
    def _():
        gust_copy(last, last).wait_recv()

    def back_copy(n, slot):
        return remote(outgoing.at[n], incoming.at[slot], back_send.at[n], back_recv.at[slot], n, s)

    def stage(n, a, b, p, q):
        first, end = max(a, HALO), min(b, HALO + STRIP)
        if first < end:
            outgoing[n, first - HALO : end - HALO, :] = jnp.where(
                lanes(end - first) < ROWS,
                p[first - a : end - a],
                pltpu.roll(q[first - a : end - a], 64, 1),
            )

    def send_back(n):
        @pl.when(t != n)
        def _():
            back_copy(n, t).start()

    for a, b in chunks(HALO, HALO + STRIP):
        stage(0, a, b, diff_p[0, PAD + a : PAD + b, :], diff_q[0, a:b, :])
    send_back(0)

    def begin(k):
        g = gusts(k)

        def finish(a, b, spring):
            p = chain_p[0, PAD + a : PAD + b, :]
            q = chain_q[a:b, :]
            coarse_q = KEEP_COARSE * q - kick[2, a:b, :] * spring
            next_q = diff_q[k, a:b, :] + coarse_q
            next_p = diff_p[k, PAD + a : PAD + b, :] + (p + COARSE * coarse_q)
            chain_q[a:b, :] = next_q
            chain_p[0, PAD + a : PAD + b, :] = next_p
            half = KEEP * q - kick[0, a:b, :] * spring + load[a:b, :] * g[0]
            pos[0, PAD + a : PAD + b, :] = p + TIME_STEP * half
            vel[0, a:b, :] = half

        return finish

    def correct(a, b, spring):
        coarse_q = KEEP_COARSE * corr_q[a:b, :] - kick[2, a:b, :] * spring
        corr_q[a:b, :] = coarse_q
        corr_p[0, PAD + a : PAD + b, :] += COARSE * coarse_q

    def end(n):
        def finish(a, b, new_p, new_q):
            new_p = new_p + corr_p[0, PAD + a : PAD + b, :]
            new_q = new_q + corr_q[a:b, :]
            corr_p[0, PAD + a : PAD + b, :] = new_p - history[n, 0, a:b, :]
            corr_q[a:b, :] = new_q - history[n, 1, a:b, :]
            closed[0, a:b, :] = new_p
            closed[1, a:b, :] = new_q

        return finish

    def turn(k, lo, stages):
        work = []
        if FINE in stages:
            n = k - FINE
            work.append((corr_p, 0, lo, correct))
            work.append((pos, FINE - 1, lo, close(FINE - 1, gusts(n), end(n))))
        for i in reversed(range(1, FINE)):
            if i in stages:
                work.append((pos, i - 1, lo, move(i - 1, i, gusts(lax.rem(k - i + tcount, tcount)), i)))
        if 0 in stages:
            work.append((chain_p, 0, lo, begin(k)))
        stencils(work)
        if 0 in stages:
            history[k, 0, lo : REGION - lo, :] = chain_p[0, PAD + lo : PAD + REGION - lo, :]
            history[k, 1, lo : REGION - lo, :] = chain_q[lo : REGION - lo, :]
        if FINE in stages:
            stage(k - FINE, HALO, HALO + STRIP, closed[0, HALO : HALO + STRIP, :], closed[1, HALO : HALO + STRIP, :])
            send_back(k - FINE)

    def turns(first, end_turn, stages):
        def step(k, carry):
            turn(k, (10 + 2 * first) // 8 * 8, stages)
            return carry

        lax.fori_loop(first, end_turn, step, 0)

    chain_p[...] = diff_p[0:1]
    chain_q[...] = diff_q[0]
    corr_p[...] = jnp.zeros_like(corr_p)
    corr_q[...] = jnp.zeros_like(corr_q)
    for k in range(1, FINE + 1):
        turn(k, (10 + 2 * k) // 8 * 8, range(k))
    turns(FINE + 1, tcount, range(FINE + 1))
    for k in range(tcount, tcount + FINE):
        turn(k, (10 + 2 * k) // 8 * 8, range(k - tcount + 1, FINE + 1))

    def place(tt, block):
        cols = pl.ds(pl.multiple_of(tt * STRIP, STRIP), STRIP)
        out[:, cols] = block.T

    place(t, outgoing[t])
    for i in range(1, tcount):
        tt = lax.rem(t + i, tcount)
        back_copy(tt, tt).wait_recv()
        place(tt, incoming[tt])

    for i in range(1, tcount + 1):
        tt = lax.rem(t + i, tcount)
        if i < tcount:
            back_copy(tt, t).wait_send()
            gust_copy(tt, t).wait_send()

            @pl.when(t < last)
            def _():
                core_copy(tt, t).wait_send()

        @pl.when(tt < last)
        def _():
            mate_copy(tt).wait_send()

        @pl.when(jnp.logical_and(t < last, has_far))
        def _():
            far_copy(tt, t).wait_send()

    coef_near.wait_send()

    @pl.when(has_far)
    def _():
        coef_away.wait_send()


def tables(tcount, scount, rows, cols):
    orders = np.arange(1, KL + 1)
    lane = np.arange(128)
    along = np.where(lane < ROWS + HALO, lane, lane - 128)
    x = np.arange(scount)[:, None] * ROWS + along[None, :]
    y = np.arange(tcount)[:, None] * STRIP - HALO + np.arange(REGION)[None, :]
    cos_x = np.zeros((scount, 8, 128), np.float32)
    cos_x[:, :KL] = np.cos(np.pi * orders[None, :, None] * ((x[:, None, :] + 0.5) / rows))
    cos_y = np.zeros((tcount, REGION, 128), np.float32)
    cos_y[:, :, :KL] = np.cos(np.pi * orders[None, None, :] * ((y[:, :, None] + 0.5) / cols))
    return cos_x, cos_y


def per_device(tcount, scount, start_state, rigidity, inv_mass, gust_load, kl_coeff, gust_history):
    rows, cols = rigidity.shape
    cos_x, cos_y = tables(tcount, scount, rows * scount, cols)
    f32 = jnp.float32
    padded = PAD + REGION + PAD
    packed = (tcount - 1) * STRIP + HALF
    vmem = pltpu.VMEM
    dma = pltpu.SemaphoreType.DMA
    hbm = pl.BlockSpec(memory_space=pltpu.HBM)
    result = pl.pallas_call(
        functools.partial(kernel, tcount, scount),
        out_shape=pltpu.VMEM((2 * rows, cols), f32),
        in_specs=[hbm] * 8,
        out_specs=pl.BlockSpec(memory_space=pltpu.VMEM),
        scratch_shapes=[
            vmem((2 * rows, cols), f32),
            vmem((3, rows, cols), f32),
            vmem((KL, KL), f32),
            vmem((1, FINE), f32),
            vmem((8, 128), f32),
            vmem((REGION, 128), f32),
            vmem((2 * HALO + tcount * STRIP, 128), f32),
            vmem((packed, 128), f32),
            vmem((2, REGION, 128), f32),
            vmem((2, HALF, 128), f32),
            vmem((tcount, REGION, 128), f32),
            vmem((tcount, REGION, 128), f32),
            vmem((tcount, HALF, 128), f32),
            vmem((tcount, 8, 128), f32),
            vmem((2, REGION, 128), f32),
            vmem((2, HALF, 128), f32),
            vmem((8, 128), f32),
            vmem((REGION, 128), f32),
            vmem((3, REGION, 128), f32),
            vmem((REGION, 128), f32),
            vmem((FINE, padded, 128), f32),
            vmem((FINE, REGION, 128), f32),
            vmem((6, padded, 128), f32),
            vmem((tcount, padded, 128), f32),
            vmem((tcount, REGION, 128), f32),
            vmem((1, padded, 128), f32),
            vmem((REGION, 128), f32),
            vmem((1, padded, 128), f32),
            vmem((REGION, 128), f32),
            vmem((2, REGION, 128), f32),
            vmem((tcount, 2, REGION, 128), f32),
            vmem((2, REGION, 128), f32),
            vmem((2, REGION, 128), f32),
            vmem((tcount, STRIP, 128), f32),
            vmem((tcount, STRIP, 128), f32),
            dma((10,)),
            dma((4, tcount)),
            dma((4, tcount)),
            dma((2,)),
            dma((2,)),
            dma((tcount,)),
            dma((tcount,)),
        ],
        compiler_params=pltpu.CompilerParams(
            collective_id=0, has_side_effects=True, vmem_limit_bytes=60 * 1024 * 1024
        ),
    )(
        start_state.reshape(2 * rows, cols),
        rigidity,
        inv_mass,
        gust_load,
        kl_coeff,
        gust_history.reshape(1, FINE),
        jnp.asarray(cos_x),
        jnp.asarray(cos_y),
    )
    return result.reshape(1, 2, rows, cols)


def solution(mesh):
    in_specs = (
        P("tm", None, "space", None),
        P("space", None),
        P("space", None),
        P("space", None),
        P(),
        P("tm"),
    )
    return jax.shard_map(
        functools.partial(per_device, mesh.shape["tm"], mesh.shape["space"]),
        mesh=mesh,
        in_specs=in_specs,
        out_specs=P("tm", None, "space", None),
        check_vma=False,
    )
```
